32 devices in a mesh: row: 8 (over y, x, core), col: 4 (over z).
Axes of the slice: x: 2, y: 2, z: 4, core: 2. Of those that a mesh axis runs over, the one named last changes fastest.
Arguments:
- amplitudes: float32 [32, 4, 512, 512], P('row', None, 'col'), may hold values from -6 to 6
- integrals: float32 [4, 512, 32, 512], P(None, 'row', 'col'), may hold values from -0.125 to 0.125
- occ_energy: float32 [32], replicated, may hold values from -1.5 to -0.3
- vir_energy: float32 [512], replicated, may hold values from 0.2 to 3
Outputs:
- update: float32 [32, 32, 512, 512], P('row', None, 'col')
The draws below stay inside these ranges and needn't reach their ends.
All inputs are finite; a program needn't handle non-finite values.
Results may differ from the reference program's by a relative error of at most 0.00007.
Values sent between devices are 32-bit elements; how exact they have to be, the bound alone decides.
No kernel may reach another device: no remote copies, remote signals or barrier semaphores. Data moves between devices by JAX's collectives and lax.ppermute only.
A program may use at most 192 MiB of HBM per device.

```python
import jax
import jax.numpy as jnp
from jax import lax

O = 32
V = 512
KOCC = 4


def shard_levels(stream_key, shape, cuts, low, top_value):
    gain = 1.0
    for position, parts in cuts:
        steps = jax.random.uniform(jax.random.fold_in(jax.random.fold_in(stream_key, 6), position), (parts,), jnp.float32, low / len(cuts), top_value / len(cuts))
        gain = gain * jnp.repeat(jnp.exp(steps), shape[position] // parts).reshape((-1,) + (1,) * (len(shape) - 1 - position))
    return gain


def centred(stream_key, shape, spread, reach, cuts=(), kind=jnp.bfloat16):
    values = jax.random.normal(stream_key, shape, jnp.float32) * spread
    if len(cuts) > 0:
        values = shard_levels(stream_key, shape, cuts, -0.22, 0.18) * values
    return jnp.clip(values, min=-reach, max=reach).astype(kind)


def setup_inputs(seed: int = 0) -> dict:
    arg_keys = jax.random.split(jax.random.key(seed), 5)
    amplitudes = centred(arg_keys[0], (O, KOCC, V, V), 1.0, 6.0, ((0, 8), (2, 4)), jnp.float32)
    integrals = centred(arg_keys[1], (KOCC, V, O, V), (KOCC * V) ** -0.5, 0.125, ((1, 8), (2, 4)), jnp.float32)
    occ_energy = jnp.clip(jax.random.uniform(arg_keys[2], (O,), jnp.float32, -1.5, -0.3), -1.5, -0.3)
    vir_energy = jnp.clip(jax.random.uniform(arg_keys[3], (V,), jnp.float32, 0.2, 3.0), 0.2, 3.0)
    return dict(amplitudes=amplitudes, integrals=integrals, occ_energy=occ_energy, vir_energy=vir_energy)


def reference(amplitudes, integrals, occ_energy, vir_energy):
    def one_row(index):
        cycle = jnp.einsum('kac,kcjb->jab', amplitudes[index], integrals, precision=lax.Precision.HIGHEST)
        denom = occ_energy[index] + occ_energy[:, None, None] - vir_energy[None, :, None] - vir_energy[None, None, :]
        return cycle / denom

    return lax.map(one_row, jnp.arange(O, dtype=jnp.int32))
```

```python
import functools

import jax
import jax.numpy as jnp
from jax import lax
from jax.experimental import pallas as pl
from jax.experimental.pallas import tpu as pltpu
from jax.sharding import PartitionSpec as P

AXES = ("row", "col")

HBM = pl.BlockSpec(memory_space=pl.ANY)
VMEM = 58 * 2**20


def streamed(amplitudes, integrals, occ_energy, vir_energy):
    planes = lax.axis_size("col")
    plane = lax.axis_index("col")
    rows_i, _, rows_a, _ = amplitudes.shape
    cols_j, cols_b = integrals.shape[2:]
    occ_i = lax.dynamic_slice_in_dim(occ_energy, lax.axis_index("row") * rows_i, rows_i, 0)
    vir_a = lax.dynamic_slice_in_dim(vir_energy, plane * rows_a, rows_a, 0)
    ring = [(z, (z + 1) % planes) for z in range(planes)]

    def step(s, carry):
        block, out = carry
        q = lax.rem(plane - s + planes, planes)
        panel = lax.all_gather(block, "row", axis=1, tiled=True)
        cycle = jnp.einsum("ikac,kcjb->ijab", amplitudes, panel, precision=lax.Precision.HIGHEST)
        occ_j = lax.dynamic_slice_in_dim(occ_energy, q * cols_j, cols_j, 0)
        denom = (
            occ_i[:, None, None, None]
            + occ_j[None, :, None, None]
            - vir_a[None, None, :, None]
            - vir_energy[None, None, None, :]
        )
        out = lax.dynamic_update_slice_in_dim(out, cycle / denom, q * cols_j, 1)
        return lax.ppermute(block, "col", ring), out

    out = jnp.zeros((rows_i, occ_energy.shape[0], rows_a, cols_b), jnp.float32)
    return lax.fori_loop(0, planes, step, (integrals, out))[1]


def split(value):
    high = value.astype(jnp.bfloat16)
    return high, (value - high.astype(jnp.float32)).astype(jnp.bfloat16)


def columns_kernel(core_ref, block, out):
    for j in range(block.shape[2]):
        to = j ^ (core_ref[0] * (block.shape[2] // 2))
        out[pl.ds(to, 1), 0] = block[0, :, j, :][None]


def columns(integrals, core):
    ks, cs, js, width = integrals.shape
    return pl.pallas_call(
        columns_kernel,
        grid_spec=pltpu.PrefetchScalarGridSpec(
            num_scalar_prefetch=1,
            grid=(ks,),
            in_specs=[pl.BlockSpec((1, cs, js, width), lambda k, _: (k, 0, 0, 0))],
            out_specs=pl.BlockSpec((js, 1, cs, width), lambda k, _: (0, k, 0, 0)),
        ),
        out_shape=jax.ShapeDtypeStruct((js, ks, cs, width), jnp.float32),
        compiler_params=pltpu.CompilerParams(vmem_limit_bytes=VMEM),
    )(core.reshape(1), integrals)


def merge_kernel(core_ref, mine, other, *refs):
    outs = refs[:-1]
    t, cs, per = pl.program_id(0), mine.shape[2], 2
    for n, out in enumerate(outs):

        @pl.when((t >= n * per) & (t < (n + 1) * per))
        def _(out=out):
            for source, at in ((mine, core_ref[0]), (other, 1 - core_ref[0])):
                out[0, :, pl.ds(pl.multiple_of(at * cs, cs), cs), :] = source[0]


def merge(ordered, other, core, room):
    parts, ks, cs, width = other.shape
    block = (1, ks, cs, width)
    pairs = parts // 2
    return pl.pallas_call(
        merge_kernel,
        grid_spec=pltpu.PrefetchScalarGridSpec(
            num_scalar_prefetch=1,
            grid=(parts,),
            in_specs=[pl.BlockSpec(block, lambda t, _: (t, 0, 0, 0))] * 2,
            out_specs=[
                pl.BlockSpec((1, ks, 2 * cs, width), lambda t, _, n=n: (jnp.clip(t - 2 * n, 0, 1), 0, 0, 0))
                for n in range(pairs)
            ]
            + [HBM],
        ),
        out_shape=[jax.ShapeDtypeStruct((2, ks, 2 * cs, width), jnp.float32)] * pairs
        + [jax.ShapeDtypeStruct(room, jnp.float32)],
        compiler_params=pltpu.CompilerParams(vmem_limit_bytes=VMEM),
    )(core.reshape(1), ordered, other)


def rows_kernel(starts, chip_ref, *refs):
    sources, (high, low) = refs[:-2], refs[-2:]
    step = pl.program_id(0)
    for source, (first, count) in zip(sources, starts):

        @pl.when((step >= first) & (step < first + count))
        def _(source=source):
            ks = source.shape[1]
            n = source.shape[3] // 4
            for m in range(4):
                at = pl.ds(pl.multiple_of((chip_ref[0] ^ m) * n, n), n)
                for k in range(ks):
                    to = pl.ds((m * ks + k) * n, n)
                    high[:, to], low[:, to] = split(source[0, k, :, at])


def rows(values, chip):
    starts, first = [], 0
    for v in values:
        starts.append((first, v.shape[0]))
        first += v.shape[0]
    _, ks, rows_a, depth = values[0].shape
    shape = jax.ShapeDtypeStruct((first * rows_a, ks * depth), jnp.bfloat16)
    return pl.pallas_call(
        functools.partial(rows_kernel, starts),
        grid_spec=pltpu.PrefetchScalarGridSpec(
            num_scalar_prefetch=1,
            grid=(first,),
            in_specs=[
                pl.BlockSpec((1, ks, rows_a, depth), lambda s, _, a=a, n=n: (jnp.clip(s - a, 0, n - 1), 0, 0, 0))
                for a, n in starts
            ],
            out_specs=[pl.BlockSpec((rows_a, ks * depth), lambda s, _: (s, 0))] * 2,
        ),
        out_shape=[shape, shape],
        compiler_params=pltpu.CompilerParams(vmem_limit_bytes=VMEM),
    )(chip.reshape(1), *values)


def product_kernel(chunks, places, mode, added, meta, occ, a_hi, a_lo, rowd, vir, *refs):
    pieces, refs = refs[: len(chunks)], refs[len(chunks) :]
    if added:
        start, refs = refs[0], refs[1:]
    if mode == "own":
        gots, refs = refs[:places], refs[places + 1 :]
        out, send, b_hi, b_lo, own, own_sem, got_sem = refs
    elif mode == "lent":
        own, send, b_hi, b_lo = refs
    else:
        part, b_hi, b_lo = refs
    block, step, tiles = pl.program_id(0), pl.program_id(1), pl.num_programs(1)
    half = tiles // 2
    ks, n = pieces[0].shape[1:3]
    tile_i = a_hi.shape[0] // 128

    def got_copy(m):
        return pltpu.make_async_copy(gots[m].at[0], out.at[:, meta[2 + 2 * m] + block], got_sem.at[m])

    def own_copy(s):
        rows_at = pl.ds(s * tile_i, tile_i)
        return pltpu.make_async_copy(own.at[rows_at], out.at[rows_at, meta[1] + block], own_sem.at[s])

    if mode == "own":

        @pl.when(step == 0)
        def _():
            for m in range(places):
                pl.when(meta[3 + 2 * m] == 1)(lambda m=m: got_copy(m).start())

    @pl.when(meta[0] == 1)
    def _():
        @pl.when(step == 0)
        def _():
            for m, piece in enumerate(pieces):
                for k in range(ks):
                    at = pl.ds((m * ks + k) * n, n)
                    b_hi[at, :], b_lo[at, :] = split(piece[0, k])

        cols = slice(0, len(chunks) * ks * n)
        dot = functools.partial(jnp.dot, preferred_element_type=jnp.float32)
        high, low = a_hi[:, cols], a_lo[:, cols]
        value = dot(low, b_hi[...]) + dot(high, b_lo[...]) + dot(high, b_hi[...])
        if added:
            value = value + start[0]
        if mode == "part":
            part[0] = value
        else:
            wide = jnp.concatenate([rowd[...]] * (value.shape[1] // 128), axis=1)
            value = value / (wide + occ[meta[1] + block] - vir[...])
            value = value.reshape(tile_i, 128, value.shape[1])

            @pl.when(step < half)
            def _():
                if mode == "lent":
                    own[0] = value
                else:
                    own[pl.ds(step * tile_i, tile_i)] = value
                    own_copy(step).start()

            @pl.when(step >= half)
            def _():
                send[0] = value

        if mode == "own":

            @pl.when(step == tiles - 1)
            def _():
                for s in range(2):
                    own_copy(s).wait()

    if mode == "own":

        @pl.when(step == tiles - 1)
        def _():
            for m in range(places):
                pl.when(meta[3 + 2 * m] == 1)(lambda m=m: got_copy(m).wait())


def product(rows_in, pieces, run, j, occ, vir, mode="own", chunks=(0, 1, 2, 3), added=None, out=None, gots=()):
    a_hi, a_lo, rowd = rows_in
    size = a_hi.shape[0]
    _, ks, n, width = pieces[0].shape
    depth = len(chunks) * ks * n
    whole = a_hi.shape[1]
    tiles, i_own = 4, size // 256
    tall = size // tiles
    tile_i = tall // 128
    assert tiles == 4 and i_own == 2 * tile_i
    block = jax.ShapeDtypeStruct((2, i_own, 128, width), jnp.float32)
    meta = jnp.stack([jnp.asarray(v, jnp.int32) for v in (run, j, *[v for _, at, keep in gots for v in (at, keep)])])
    args = [meta, occ, a_hi, a_lo, rowd, vir, *pieces]
    if chunks[0] == 0:
        a_spec = pl.BlockSpec((tall, whole), lambda b, s, *_: (s, 0))
    else:
        a_spec = pl.BlockSpec((tall, depth), lambda b, s, *_: (s, chunks[0]))
    specs = [a_spec, a_spec, pl.BlockSpec((tall, 128), lambda b, s, *_: (s, 0))]
    specs += [pl.BlockSpec(vir.shape, lambda b, s, *_: (0, 0))]
    specs += [pl.BlockSpec((1, ks, n, width), lambda b, s, *_: (b, 0, 0, 0))] * len(pieces)
    part_spec = pl.BlockSpec((1, tall, width), lambda b, s, *_: (b, s, 0))
    if added is not None:
        args.append(added)
        specs.append(part_spec)
    own_spec = pl.BlockSpec((1, tile_i, 128, width), lambda b, s, *_: (b, jnp.minimum(s, 1), 0, 0))
    send_spec = pl.BlockSpec((1, tile_i, 128, width), lambda b, s, *_: (b, jnp.maximum(s - 2, 0), 0, 0))
    scratch = [pltpu.VMEM((depth, width), jnp.bfloat16)] * 2
    alias = {}
    if mode == "own":
        args += [*[g for g, _, _ in gots], out]
        specs += [pl.BlockSpec((1, i_own, 128, width), lambda b, s, *_: (b, 0, 0, 0))] * len(gots) + [HBM]
        alias = {len(args) - 1: 0}
        scratch += [pltpu.VMEM(block.shape[1:], jnp.float32)]
        scratch += [pltpu.SemaphoreType.DMA((2,)), pltpu.SemaphoreType.DMA((max(len(gots), 1),))]
        out_specs, out_shape = [HBM, send_spec], [jax.ShapeDtypeStruct(out.shape, out.dtype), block]
    elif mode == "lent":
        out_specs, out_shape = [own_spec, send_spec], [block, block]
    else:
        out_specs, out_shape = part_spec, jax.ShapeDtypeStruct((2, size, width), jnp.float32)
    return pl.pallas_call(
        functools.partial(product_kernel, chunks, len(gots), mode, added is not None),
        grid_spec=pltpu.PrefetchScalarGridSpec(
            num_scalar_prefetch=2, grid=(2, tiles), in_specs=specs, out_specs=out_specs, scratch_shapes=scratch
        ),
        out_shape=out_shape,
        input_output_aliases=alias,
        compiler_params=pltpu.CompilerParams(vmem_limit_bytes=VMEM),
        cost_estimate=pl.CostEstimate(
            flops=12 * size * depth * width, bytes_accessed=8 * size * (depth + width) + 8 * depth * width, transcendentals=0
        ),
    )(*args)


def place_kernel(count, meta, *refs):
    gots, out, sem = refs[:count], refs[count + 1], refs[count + 2]
    for act in ("start", "wait"):
        for n in range(count):
            copy = pltpu.make_async_copy(gots[n].at[0], out.at[:, meta[2 * n] + pl.program_id(0)], sem.at[n])
            pl.when(meta[2 * n + 1] == 1)(getattr(copy, act))


def place(out, gots):
    meta = jnp.stack([jnp.asarray(v, jnp.int32) for _, at, keep in gots for v in (at, keep)])
    return pl.pallas_call(
        functools.partial(place_kernel, len(gots)),
        grid_spec=pltpu.PrefetchScalarGridSpec(
            num_scalar_prefetch=1,
            grid=(2,),
            in_specs=[pl.BlockSpec((1, *g.shape[1:]), lambda b, _: (b, 0, 0, 0)) for g, _, _ in gots] + [HBM],
            out_specs=HBM,
            scratch_shapes=[pltpu.SemaphoreType.DMA((len(gots),))],
        ),
        out_shape=jax.ShapeDtypeStruct(out.shape, out.dtype),
        input_output_aliases={len(gots) + 1: 0},
        compiler_params=pltpu.CompilerParams(vmem_limit_bytes=VMEM),
    )(meta, *[g for g, _, _ in gots], out)


def hop(value, mask=0, planes=None, core=0):
    planes = {z: z for z in range(4)} if planes is None else planes
    flip = 2 * mask + core
    pairs = [(r * 4 + z, (r ^ flip) * 4 + w) for r in range(8) for z, w in planes.items()]
    return lax.ppermute(value, AXES, pairs)


def together(values):
    return lax.optimization_barrier(values)


def body(amplitudes, integrals, occ_energy, vir_energy):
    row, plane = lax.axis_index("row"), lax.axis_index("col")
    core, chip = lax.rem(row, 2), lax.div(row, 2)
    rows_i, ks, rows_a, depth = amplitudes.shape
    cols_j, cols_b = integrals.shape[2:]
    parts = cols_j // 2
    swap, cross = {0: 1, 1: 0, 2: 3, 3: 2}, {1: 2, 2: 1}
    is_end = (plane == 0) | (plane == 3)
    is_mid = ~is_end
    vir = vir_energy.reshape(1, -1)

    def share(plane_of):
        occ = [lax.dynamic_slice_in_dim(occ_energy, r * rows_i, rows_i, 0) for r in (row, row ^ 1)]
        part = lax.dynamic_slice_in_dim(vir_energy, plane_of * rows_a, rows_a, 0)
        rowd = (jnp.concatenate(occ)[:, None] - part[None, :]).reshape(-1, 1)
        return jnp.broadcast_to(rowd, (rowd.shape[0], 128))

    def column(w, pair, of_core):
        return (plane ^ w) * cols_j + of_core * parts + 2 * pair

    def either(at_end, at_mid):
        return jnp.where(is_end, at_end, at_mid)

    def along(x, y, z, mid=None, flip=0):
        got = [hop(x, mask=1), hop(y, mask=2), hop(z, planes=swap, core=flip)]
        return got + [hop(mid, planes=cross)] if mid is not None else got

    ordered = columns(integrals, core)
    room = (rows_i, occ_energy.shape[0], rows_a, cols_b)
    a0, b0, out = merge(ordered, hop(ordered[parts:], core=1), core, room)
    state = dict(out=out, gots=[], sends=[])

    def work(name, rows_in, pieces, w, pair, run=1, **how):
        state["out"], send = product(
            rows_in, pieces, run, column(w, pair, core), occ_energy, vir, out=state["out"], gots=state["gots"], **how
        )
        state["gots"] = []
        state["sends"].append((send, column(w, pair, 1 - core), run))

    def exchange(count=2):
        now, state["sends"] = state["sends"][:count], state["sends"][count:]
        return [(hop(v, core=1), at, keep) for v, at, keep in now]

    def end_round(values, moved=()):
        gots, sends = state["gots"] + list(moved), state["sends"]
        values, new_gots, new_sends, state["out"] = together(
            (values, [g[0] for g in gots], [s[0] for s in sends], state["out"])
        )
        state["gots"] = [(v, *g[1:]) for v, g in zip(new_gots, gots)]
        state["sends"] = [(v, *s[1:]) for v, s in zip(new_sends, sends)]
        return values

    a_other = hop(amplitudes, core=1)
    a0x, b0y, a1, a3m = along(a0, b0, a0, a0)
    v = end_round((amplitudes, a_other, a0, b0, a0x, b0y, a1, a3m))
    amplitudes, a_other, a0, b0, a0x, b0y, a1, a3m = v
    b0x, a0y, ab, a2m = along(b0, a0, either(b0, a3m), a1)
    here = rows([amplitudes, a_other], chip)
    v = end_round((amplitudes, here, a0, b0, a0x, b0y, a1, a3m, b0x, a0y, ab, a2m))
    amplitudes, here, a0, b0, a0x, b0y, a1, a3m, b0x, a0y, ab, a2m = v
    here = (*here, share(plane))
    b0d, a0d, first, b3m = along(b0y, a0x, either(amplitudes[:2], a2m), b0)
    first_other = hop(first, core=1)
    v = end_round((amplitudes, here, a0, b0, a0x, b0y, a1, a3m, b0x, a0y, ab, a2m, b0d, a0d, first, first_other, b3m))
    amplitudes, here, a0, b0, a0x, b0y, a1, a3m, b0x, a0y, ab, a2m, b0d, a0d, first, first_other, b3m = v
    e3, e6 = either(ab, a2m), either(first, ab)
    e3x, e6y, second, b2m = along(e3, e6, either(amplitudes[2:], b3m), ab)
    work("k1", here, (a0, a0x, a0y, a0d), 0, 0)
    work("k2", here, (b0, b0x, b0y, b0d), 0, 1)
    second, state["out"] = together((second, state["out"]))
    second_other = hop(second, core=1)
    v = end_round((here, a0, b0, a0x, b0y, a1, a3m, b0x, a0y, b2m, b0d, a0d, first, first_other, second, second_other, b3m, e3, e6, e3x, e6y))
    here, a0, b0, a0x, b0y, a1, a3m, b0x, a0y, b2m, b0d, a0d, first, first_other, second, second_other, b3m, e3, e6, e3x, e6y = v
    near = (*rows([first, second, first_other, second_other], chip), share(plane ^ 1))
    e4 = either(second, b2m)
    moved = exchange(1)
    e6x, e3y, third, g3x = along(e6, e3, either(a0x, b2m), a0x)
    s_a, l_a = product(near, (a0, a0x, a0y, a0d), is_mid, column(0, 0, core), occ_energy, vir, mode="lent")
    v = end_round((here, near, b0, b0y, a1, a3m, b0x, a0y, b0d, a0d, b3m, e3, e6, e3x, e6y, e4, e6x, e3y, third, g3x, s_a, l_a), moved)
    here, near, b0, b0y, a1, a3m, b0x, a0y, b0d, a0d, b3m, e3, e6, e3x, e6y, e4, e6x, e3y, third, g3x, s_a, l_a = v
    e5 = either(third, b3m)
    moved = exchange(1)
    e6d, e3d, fourth, g3y = along(e6y, e3x, either(a0y, s_a), a0y)
    s_b, l_b = product(near, (b0, b0x, b0y, b0d), is_mid, column(0, 1, core), occ_energy, vir, mode="lent")
    v = end_round((here, a1, a3m, a0d, e3, e6, e3x, e6y, e4, e5, e6x, e3y, third, g3x, e6d, e3d, fourth, g3y, l_a, s_b, l_b), moved)
    here, a1, a3m, a0d, e3, e6, e3x, e6y, e4, e5, e6x, e3y, third, g3x, e6d, e3d, fourth, g3y, l_a, s_b, l_b = v
    state["gots"].append((fourth, column(1, 0, core), is_end))
    e4x, e5y, fifth, g3d = along(e4, e5, either(a0d, s_b), a0d)
    work("k3", here, (e3, e3x, e3y, e3d), 2, 0)
    work("k6", here, (e6, e6x, e6y, e6d), either(3, 1), either(0, 1))
    v = end_round((here, a1, a3m, e4, e5, third, fourth, fifth, g3x, g3y, g3d, l_a, l_b, e4x, e5y))
    here, a1, a3m, e4, e5, third, fourth, fifth, g3x, g3y, g3d, l_a, l_b, e4x, e5y = v
    state["gots"].append((fifth, column(1, 1, core), is_end))
    moved = exchange()
    e5x, e4y, sixth = along(e5, e4, l_a, flip=1)
    work("g1", here, (a1, third, fourth, fifth), 1, 0, is_mid)
    work("g3", here, (a3m, g3x, g3y, g3d), 3, 0, is_mid)
    moved.append((sixth, column(1, 0, 1 - core), is_end))
    v = end_round((here, e4, e5, l_b, e4x, e5y, e5x, e4y), moved)
    here, e4, e5, l_b, e4x, e5y, e5x, e4y = v
    moved = exchange()
    e5d, e4d, seventh = along(e5y, e4x, l_b, flip=1)
    p4 = product(here, (e4, e4x, e4y), 1, column(2, 1, core), occ_energy, vir, mode="part", chunks=(0, 1, 2))
    p5 = product(here, (e5, e5x, e5y), 1, column(3, 1, core), occ_energy, vir, mode="part", chunks=(0, 1, 2))
    moved.append((seventh, column(1, 1, 1 - core), is_end))
    here, e4d, e5d, p4, p5 = end_round((here, e4d, e5d, p4, p5), moved)
    work("k4", here, (e4d,), 2, 1, chunks=(3,), added=p4)
    moved = exchange()
    work("k5", here, (e5d,), 3, 1, chunks=(3,), added=p5)
    return place(state["out"], state["gots"] + moved + exchange())


def solution(mesh):
    planned = mesh.shape["row"] == 8 and mesh.shape["col"] == 4
    return jax.shard_map(
        body if planned else streamed,
        mesh=mesh,
        in_specs=(P("row", None, "col", None), P(None, "row", "col", None), P(), P()),
        out_specs=P("row", None, "col", None),
        check_vma=False,
    )
```

```python
import functools

import jax
import jax.numpy as jnp
from jax import lax
from jax.experimental import pallas as pl
from jax.experimental.pallas import tpu as pltpu
from jax.sharding import PartitionSpec as P

AXES = ("row", "col")

HBM = pl.BlockSpec(memory_space=pl.ANY)
VMEM = 58 * 2**20


def streamed(amplitudes, integrals, occ_energy, vir_energy):
    planes = lax.axis_size("col")
    plane = lax.axis_index("col")
    rows_i, _, rows_a, _ = amplitudes.shape
    cols_j, cols_b = integrals.shape[2:]
    occ_i = lax.dynamic_slice_in_dim(occ_energy, lax.axis_index("row") * rows_i, rows_i, 0)
    vir_a = lax.dynamic_slice_in_dim(vir_energy, plane * rows_a, rows_a, 0)
    ring = [(z, (z + 1) % planes) for z in range(planes)]

    def step(s, carry):
        block, out = carry
        q = lax.rem(plane - s + planes, planes)
        panel = lax.all_gather(block, "row", axis=1, tiled=True)
        cycle = jnp.einsum("ikac,kcjb->ijab", amplitudes, panel, precision=lax.Precision.HIGHEST)
        occ_j = lax.dynamic_slice_in_dim(occ_energy, q * cols_j, cols_j, 0)
        denom = (
            occ_i[:, None, None, None]
            + occ_j[None, :, None, None]
            - vir_a[None, None, :, None]
            - vir_energy[None, None, None, :]
        )
        out = lax.dynamic_update_slice_in_dim(out, cycle / denom, q * cols_j, 1)
        return lax.ppermute(block, "col", ring), out

    out = jnp.zeros((rows_i, occ_energy.shape[0], rows_a, cols_b), jnp.float32)
    return lax.fori_loop(0, planes, step, (integrals, out))[1]


def split(value):
    high = value.astype(jnp.bfloat16)
    return high, (value - high.astype(jnp.float32)).astype(jnp.bfloat16)


def columns_kernel(pair, core_ref, block, mine, other):
    half = block.shape[2] // 2
    for which in range(2):

        @pl.when(core_ref[0] == which)
        def _(which=which):
            for t in range(2):
                mine[t, 0] = block[0, :, which * half + 2 * pair + t, :]
                other[t, 0] = block[0, :, (1 - which) * half + 2 * pair + t, :]


def columns(integrals, core, pair):
    ks, cs, js, width = integrals.shape
    return pl.pallas_call(
        functools.partial(columns_kernel, pair),
        grid_spec=pltpu.PrefetchScalarGridSpec(
            num_scalar_prefetch=1,
            grid=(ks,),
            in_specs=[pl.BlockSpec((1, cs, js, width), lambda k, _: (k, 0, 0, 0))],
            out_specs=[pl.BlockSpec((2, 1, cs, width), lambda k, _: (0, k, 0, 0))] * 2,
        ),
        out_shape=[jax.ShapeDtypeStruct((2, ks, cs, width), jnp.float32)] * 2,
        compiler_params=pltpu.CompilerParams(vmem_limit_bytes=VMEM),
    )(core.reshape(1), integrals)


def merge_kernel(core_ref, mine, other, out, *room):
    cs = mine.shape[2]
    for source, at in ((mine, core_ref[0]), (other, 1 - core_ref[0])):
        out[0, :, pl.ds(pl.multiple_of(at * cs, cs), cs), :] = source[0]


def merge(mine, other, core, room=None):
    _, ks, cs, width = other.shape
    block = (1, ks, cs, width)
    return pl.pallas_call(
        merge_kernel,
        grid_spec=pltpu.PrefetchScalarGridSpec(
            num_scalar_prefetch=1,
            grid=(2,),
            in_specs=[pl.BlockSpec(block, lambda t, _: (t, 0, 0, 0))] * 2,
            out_specs=[pl.BlockSpec((1, ks, 2 * cs, width), lambda t, _: (t, 0, 0, 0))] + [HBM] * (room is not None),
        ),
        out_shape=[jax.ShapeDtypeStruct((2, ks, 2 * cs, width), jnp.float32)]
        + [jax.ShapeDtypeStruct(r, jnp.float32) for r in [room] if r],
        compiler_params=pltpu.CompilerParams(vmem_limit_bytes=VMEM),
    )(core.reshape(1), mine, other)


def rows_kernel(starts, chip_ref, *refs):
    sources, (high, low) = refs[:-2], refs[-2:]
    step = pl.program_id(0)
    for source, (first, count) in zip(sources, starts):

        @pl.when((step >= first) & (step < first + count))
        def _(source=source):
            ks = source.shape[1]
            n = source.shape[3] // 4
            for m in range(4):
                at = pl.ds(pl.multiple_of((chip_ref[0] ^ m) * n, n), n)
                for k in range(ks):
                    to = pl.ds((m * ks + k) * n, n)
                    high[:, to], low[:, to] = split(source[0, k, :, at])


def rows(values, chip):
    starts, first = [], 0
    for v in values:
        starts.append((first, v.shape[0]))
        first += v.shape[0]
    _, ks, rows_a, depth = values[0].shape
    shape = jax.ShapeDtypeStruct((first * rows_a, ks * depth), jnp.bfloat16)
    return pl.pallas_call(
        functools.partial(rows_kernel, starts),
        grid_spec=pltpu.PrefetchScalarGridSpec(
            num_scalar_prefetch=1,
            grid=(first,),
            in_specs=[
                pl.BlockSpec((1, ks, rows_a, depth), lambda s, _, a=a, n=n: (jnp.clip(s - a, 0, n - 1), 0, 0, 0))
                for a, n in starts
            ],
            out_specs=[pl.BlockSpec((rows_a, ks * depth), lambda s, _: (s, 0))] * 2,
        ),
        out_shape=[shape, shape],
        compiler_params=pltpu.CompilerParams(vmem_limit_bytes=VMEM),
    )(chip.reshape(1), *values)


def each_place(act, gots, blocks, out, keys, at, block, sem):
    for n, got in enumerate(gots):

        @pl.when((keys[at] == 1) & (block < blocks[n]))
        def _(n=n, got=got, at=at):
            copy = pltpu.make_async_copy(got.at[0], out.at[:, keys[at + 1 + block]], sem.at[n])
            getattr(copy, act)()

        at += 1 + blocks[n]


def place_keys(gots):
    return [v for _, js, keep in gots for v in (keep, *js)]


def place_spec(got):
    last = got.shape[0] - 1
    return pl.BlockSpec((1, *got.shape[1:]), lambda b, *_: (jnp.minimum(b, last), 0, 0, 0))


def product_kernel(chunks, sets, blocks, mode, added, keys, occ, a_hi, a_lo, rowd, vir, *refs):
    pieces, refs = refs[: sets * len(chunks)], refs[sets * len(chunks) :]
    if added:
        start, refs = refs[0], refs[1:]
    places_here = mode in ("own", "mine")
    if places_here:
        gots, refs = refs[: len(blocks)], refs[len(blocks) + 1 :]
        out, *send, b_hi, b_lo, own, own_sem, got_sem = refs
        send = send[0] if send else None
    elif mode == "send":
        send, b_hi, b_lo = refs
    elif mode == "lent":
        own, send, b_hi, b_lo = refs
    else:
        part, b_hi, b_lo = refs
    block, step, tiles = pl.program_id(0), pl.program_id(1), pl.num_programs(1)
    own_at, send_at = {"mine": (0, None), "send": (None, 0)}.get(mode, (0, 1))
    ks, n = pieces[0].shape[1:3]
    tile_i = a_hi.shape[0] // 128
    column = keys[1 + block]

    def own_copy():
        return pltpu.make_async_copy(own, out.at[:, column], own_sem.at[0])

    def places(act):
        each_place(act, gots, blocks, out, keys, 1 + 2 * sets, block, got_sem)

    if places_here:
        pl.when(step == 0)(lambda: places("start"))

    @pl.when(keys[0] == 1)
    def _():
        for one in range(sets):

            @pl.when((step == 0) & (block >= 2 * one) & (block < 2 * one + 2))
            def _(one=one):
                for m in range(len(chunks)):
                    for k in range(ks):
                        at = pl.ds((m * ks + k) * n, n)
                        b_hi[at, :], b_lo[at, :] = split(pieces[one * len(chunks) + m][0, k])

        cols = slice(0, len(chunks) * ks * n)
        dot = functools.partial(jnp.dot, preferred_element_type=jnp.float32)
        high, low = a_hi[:, cols], a_lo[:, cols]
        value = dot(low, b_hi[...]) + dot(high, b_lo[...]) + dot(high, b_hi[...])
        if added:
            value = value + start[0]
        if mode == "part":
            part[0] = value
        else:
            wide = jnp.concatenate([rowd[...]] * (value.shape[1] // 128), axis=1)
            value = value / (wide + occ[column] - vir[...])
            value = value.reshape(tile_i, 128, value.shape[1])
            if own_at is not None:

                @pl.when(step == own_at)
                def _():
                    if mode == "lent":
                        own[0] = value
                    else:
                        own[...] = value
                        own_copy().start()

            if send_at is not None:

                @pl.when(step == send_at)
                def _():
                    send[0] = value

        if places_here:
            pl.when(step == tiles - 1)(lambda: own_copy().wait())

    if places_here:
        pl.when(step == tiles - 1)(lambda: places("wait"))


def product(rows_in, sets, run, js, occ, vir, mode="own", chunks=(0, 1, 2, 3), added=None, out=None, gots=()):
    a_hi, a_lo, rowd = rows_in
    size, whole = a_hi.shape
    _, ks, n, width = sets[0][0].shape
    depth = len(chunks) * ks * n
    count = 2 * len(sets)
    i_own = size // 256
    tall = size // 2
    first, tiles = {"mine": (0, 1), "send": (1, 1)}.get(mode, (0, 2))
    block = jax.ShapeDtypeStruct((count, i_own, 128, width), jnp.float32)
    block_spec = pl.BlockSpec((1, i_own, 128, width), lambda b, s, *_: (b, 0, 0, 0))
    part_spec = pl.BlockSpec((1, tall, width), lambda b, s, *_: (b, s + first, 0))
    keys = jnp.stack([jnp.asarray(v, jnp.int32) for v in (run, *js, *place_keys(gots))])
    args = [keys, occ, a_hi, a_lo, rowd, vir]
    if chunks[0] == 0:
        a_spec = pl.BlockSpec((tall, whole), lambda b, s, *_: (s + first, 0))
    else:
        a_spec = pl.BlockSpec((tall, depth), lambda b, s, *_: (s + first, chunks[0]))
    specs = [a_spec, a_spec, pl.BlockSpec((tall, 128), lambda b, s, *_: (s + first, 0))]
    specs += [pl.BlockSpec(vir.shape, lambda b, s, *_: (0, 0))]
    for one, pieces in enumerate(sets):
        args += pieces
        specs += [
            pl.BlockSpec((1, ks, n, width), lambda b, s, *_, one=one: (jnp.clip(b - 2 * one, 0, 1), 0, 0, 0))
        ] * len(pieces)
    if added is not None:
        args.append(added)
        specs.append(part_spec)
    scratch = [pltpu.VMEM((depth, width), jnp.bfloat16)] * 2
    alias = {}
    if mode in ("own", "mine"):
        args += [*[g for g, _, _ in gots], out]
        specs += [place_spec(g) for g, _, _ in gots] + [HBM]
        alias = {len(args) - 1: 0}
        scratch += [pltpu.VMEM(block.shape[1:], jnp.float32)]
        scratch += [pltpu.SemaphoreType.DMA((1,)), pltpu.SemaphoreType.DMA((max(len(gots), 1),))]
        out_specs, out_shape = [HBM], [jax.ShapeDtypeStruct(out.shape, out.dtype)]
        if mode == "own":
            out_specs, out_shape = out_specs + [block_spec], out_shape + [block]
    elif mode == "send":
        out_specs, out_shape = block_spec, block
    elif mode == "lent":
        out_specs, out_shape = [block_spec, block_spec], [block, block]
    else:
        out_specs, out_shape = part_spec, jax.ShapeDtypeStruct((count, size, width), jnp.float32)
    return pl.pallas_call(
        functools.partial(product_kernel, chunks, len(sets), [g.shape[0] for g, _, _ in gots], mode, added is not None),
        grid_spec=pltpu.PrefetchScalarGridSpec(
            num_scalar_prefetch=2, grid=(count, tiles), in_specs=specs, out_specs=out_specs, scratch_shapes=scratch
        ),
        out_shape=out_shape,
        input_output_aliases=alias,
        compiler_params=pltpu.CompilerParams(vmem_limit_bytes=VMEM),
        cost_estimate=pl.CostEstimate(
            flops=6 * count * size * depth * width // (2 // tiles),
            bytes_accessed=4 * count * (size * (depth + width) + depth * width),
            transcendentals=0,
        ),
    )(*args)


def place_kernel(blocks, keys, *refs):
    gots, out, sem = refs[: len(blocks)], refs[len(blocks) + 1], refs[len(blocks) + 2]
    for act in ("start", "wait"):
        each_place(act, gots, blocks, out, keys, 0, pl.program_id(0), sem)


def place(out, gots):
    keys = jnp.stack([jnp.asarray(v, jnp.int32) for v in place_keys(gots)])
    blocks = [g.shape[0] for g, _, _ in gots]
    return pl.pallas_call(
        functools.partial(place_kernel, blocks),
        grid_spec=pltpu.PrefetchScalarGridSpec(
            num_scalar_prefetch=1,
            grid=(max(blocks),),
            in_specs=[place_spec(g) for g, _, _ in gots] + [HBM],
            out_specs=HBM,
            scratch_shapes=[pltpu.SemaphoreType.DMA((len(gots),))],
        ),
        out_shape=jax.ShapeDtypeStruct(out.shape, out.dtype),
        input_output_aliases={len(gots) + 1: 0},
        compiler_params=pltpu.CompilerParams(vmem_limit_bytes=VMEM),
    )(keys, *[g for g, _, _ in gots], out)


def hop(value, mask=0, planes=None, core=0):
    planes = {z: z for z in range(4)} if planes is None else planes
    flip = 2 * mask + core
    pairs = [(r * 4 + z, (r ^ flip) * 4 + w) for r in range(8) for z, w in planes.items()]
    return lax.ppermute(value, AXES, pairs)


def hop_middle(value):
    pairs = [(r * 4 + z, r * 4 + 3 - z) for r in range(8) for z in (1, 2)]
    pairs += [(r * 4 + z, (r ^ 1) * 4 + z) for r in range(8) for z in (0, 3)]
    return lax.ppermute(value, AXES, pairs)


def together(values):
    return lax.optimization_barrier(values)


def body(amplitudes, integrals, occ_energy, vir_energy):
    row, plane = lax.axis_index("row"), lax.axis_index("col")
    core, chip = lax.rem(row, 2), lax.div(row, 2)
    rows_i, ks, rows_a, depth = amplitudes.shape
    cols_j, cols_b = integrals.shape[2:]
    parts = cols_j // 2
    swap = {0: 1, 1: 0, 2: 3, 3: 2}
    is_end = (plane == 0) | (plane == 3)
    is_mid = ~is_end
    vir = vir_energy.reshape(1, -1)

    def share(plane_of):
        occ = [lax.dynamic_slice_in_dim(occ_energy, r * rows_i, rows_i, 0) for r in (row, row ^ 1)]
        part = lax.dynamic_slice_in_dim(vir_energy, plane_of * rows_a, rows_a, 0)
        rowd = (jnp.concatenate(occ)[:, None] - part[None, :]).reshape(-1, 1)
        return jnp.broadcast_to(rowd, (rowd.shape[0], 128))

    def column(w, pair, of_core):
        return (plane ^ w) * cols_j + of_core * parts + 2 * pair

    def either(at_end, at_mid):
        return jnp.where(is_end, at_end, at_mid)

    def along(x, y, z, mid=None, flip=0):
        got = [hop_middle(mid)] if mid is not None else []
        return [hop(x, mask=1), hop(y, mask=2), hop(z, planes=swap, core=flip)] + got

    room = (rows_i, occ_energy.shape[0], rows_a, cols_b)
    mine, other = columns(integrals, core, 0)
    a0, out = merge(mine, hop(other, core=1), core, room)
    state = dict(out=out, gots=[], sends=[])

    def columns_of(w, pair, of_core):
        at = column(w, pair, of_core)
        return [at, at + 1]

    def work(rows_in, sets, where, run=1, **how):
        js = [j for w, pair in where for j in columns_of(w, pair, core)]
        state["out"], send = product(rows_in, sets, run, js, occ_energy, vir, out=state["out"], gots=state["gots"], **how)
        state["gots"] = []
        state["sends"].append((send, [j for w, pair in where for j in columns_of(w, pair, 1 - core)], run))

    def exchange():
        now, state["sends"] = state["sends"], []
        return [(hop(v, core=1), js, keep) for v, js, keep in now]

    def end_round(values, moved=()):
        gots, sends = state["gots"] + list(moved), state["sends"]
        values, new_gots, new_sends, state["out"] = together(
            (values, [g[0] for g in gots], [s[0] for s in sends], state["out"])
        )
        state["gots"] = [(v, *g[1:]) for v, g in zip(new_gots, gots)]
        state["sends"] = [(v, *s[1:]) for v, s in zip(new_sends, sends)]
        return values

    a0x, a0y, a1, a3m = along(a0, a0, a0, a0)
    mine, other = columns(integrals, core, 1)
    (b0,) = merge(mine, hop(other, core=1), core)
    z = either(b0, a3m)
    v = end_round((amplitudes, a0, b0, a0x, a0y, a1, a3m, z))
    amplitudes, a0, b0, a0x, a0y, a1, a3m, z = v
    a_other = hop(amplitudes, core=1)
    a0d, b0y, ab, a2m = along(a0y, b0, z, a1)
    z = either(amplitudes[:2], a2m)
    e3 = either(ab, a2m)
    v = end_round((amplitudes, a_other, a0, b0, a0x, a0y, a0d, a1, a3m, b0y, ab, e3, z))
    amplitudes, a_other, a0, b0, a0x, a0y, a0d, a1, a3m, b0y, ab, e3, z = v
    b0x, e3y, first, b3m = along(b0, e3, z, b0)
    here = (*rows([amplitudes, a_other], chip), share(plane))
    work(here, [(a0, a0x, a0y, a0d)], [(0, 0)])
    z = either(amplitudes[2:], b3m)
    first, state["out"] = together((first, state["out"]))
    first_other = hop(first, core=1)
    v = end_round((here, a0, b0, a0x, a0y, a0d, a1, a3m, b0x, b0y, ab, e3, e3y, first, first_other, b3m, z))
    here, a0, b0, a0x, a0y, a0d, a1, a3m, b0x, b0y, ab, e3, e3y, first, first_other, b3m, z = v
    moved = exchange()
    e3x, b0d, second, b2m = along(e3, b0x, z, ab)
    e6 = either(first, ab)
    z = either(a0x, b2m)
    v = (here, a0, b0, a0x, a0y, a0d, a1, a3m, b0x, b0y, b0d, b2m, e3, e3x, e3y, e6, first, first_other, second, b3m, z)
    v = end_round(v, moved)
    here, a0, b0, a0x, a0y, a0d, a1, a3m, b0x, b0y, b0d, b2m, e3, e3x, e3y, e6, first, first_other, second, b3m, z = v
    second_other = hop(second, core=1)
    e6x, e6y, third, g3x = along(e6, e6, z, a0x)
    e4, first = together((either(second, b2m), first))
    near = (*rows([first, second, first_other, second_other], chip), share(plane ^ 1))
    s_a, l_a = product(near, [(a0, a0x, a0y, a0d)], is_mid, columns_of(0, 0, core), occ_energy, vir, mode="lent")
    z = either(a0y, s_a)
    v = (here, near, a1, a3m, b0, b0x, b0y, b0d, a0y, a0d, b3m, e3, e3x, e3y, e4, e6, e6x, e6y, third, g3x, l_a, z)
    v = end_round(v)
    here, near, a1, a3m, b0, b0x, b0y, b0d, a0y, a0d, b3m, e3, e3x, e3y, e4, e6, e6x, e6y, third, g3x, l_a, z = v
    e3d, e6d, fourth, g3y = along(e3y, e6x, z, a0y)
    e5, near = together((either(third, b3m), near))
    s_b, l_b = product(near, [(b0, b0x, b0y, b0d)], is_mid, columns_of(0, 1, core), occ_energy, vir, mode="lent")
    z, here = together((either(a0d, s_b), here))
    work(here, [(b0, b0x, b0y, b0d)], [(0, 1)])
    v = (here, a1, a3m, a0d, e3, e3x, e3y, e3d, e4, e5, e6, e6x, e6y, e6d, third, fourth, g3x, g3y, l_a, l_b, z)
    v = end_round(v)
    here, a1, a3m, a0d, e3, e3x, e3y, e3d, e4, e5, e6, e6x, e6y, e6d, third, fourth, g3x, g3y, l_a, l_b, z = v
    state["gots"].append((fourth, columns_of(1, 0, core), is_end))
    moved = exchange()
    e4x, e4y, fifth, g3d = along(e4, e4, z, a0d)
    work(here, [(e3, e3x, e3y, e3d), (e6, e6x, e6y, e6d)], [(2, 0), (either(3, 1), either(0, 1))])
    v = end_round((here, a1, a3m, e4, e4x, e4y, e5, third, fourth, fifth, g3x, g3y, g3d, l_a, l_b), moved)
    here, a1, a3m, e4, e4x, e4y, e5, third, fourth, fifth, g3x, g3y, g3d, l_a, l_b = v
    state["gots"].append((fifth, columns_of(1, 1, core), is_end))
    moved = exchange()
    e5x, e5y, sixth = along(e5, e5, l_a, flip=1)
    work(here, [(a1, third, fourth, fifth), (a3m, g3x, g3y, g3d)], [(1, 0), (3, 0)], is_mid)
    moved.append((sixth, columns_of(1, 0, 1 - core), is_end))
    v = end_round((here, e4, e4x, e4y, e5, e5x, e5y, l_b), moved)
    here, e4, e4x, e4y, e5, e5x, e5y, l_b = v
    moved = exchange()
    e4d, e5d, seventh = along(e4y, e5x, l_b, flip=1)
    last = [(2, 1), (3, 1)]
    js = [j for w, pair in last for j in columns_of(w, pair, core)]
    sums = product(
        here, [(e4, e4x, e4y), (e5, e5x, e5y)], 1, js, occ_energy, vir, mode="part", chunks=(0, 1, 2)
    )
    sums, state["out"] = together((sums, state["out"]))
    state["out"], state["gots"] = place(state["out"], state["gots"] + moved), []
    here, e4d, e5d, sums = end_round((here, e4d, e5d, sums), [(seventh, columns_of(1, 1, 1 - core), is_end)])
    how = dict(chunks=(3,), added=sums)
    send = product(here, [(e4d,), (e5d,)], 1, js, occ_energy, vir, mode="send", **how)
    got = hop(send, core=1)
    (out,) = product(
        here, [(e4d,), (e5d,)], 1, js, occ_energy, vir, mode="mine", out=state["out"], gots=state["gots"], **how
    )
    return place(out, [(got, [j for w, pair in last for j in columns_of(w, pair, 1 - core)], 1)])


def solution(mesh):
    planned = mesh.shape["row"] == 8 and mesh.shape["col"] == 4
    return jax.shard_map(
        body if planned else streamed,
        mesh=mesh,
        in_specs=(P("row", None, "col", None), P(None, "row", "col", None), P(), P()),
        out_specs=P("row", None, "col", None),
        check_vma=False,
    )
```

```python
import functools

import jax
import jax.numpy as jnp
from jax import lax
from jax.experimental import pallas as pl
from jax.experimental.pallas import tpu as pltpu
from jax.sharding import PartitionSpec as P

AXES = ("row", "col")

HBM = pl.BlockSpec(memory_space=pl.ANY)
VMEM = 44 * 2**20


def streamed(amplitudes, integrals, occ_energy, vir_energy):
    planes = lax.axis_size("col")
    plane = lax.axis_index("col")
    rows_i, _, rows_a, _ = amplitudes.shape
    cols_j, cols_b = integrals.shape[2:]
    occ_i = lax.dynamic_slice_in_dim(occ_energy, lax.axis_index("row") * rows_i, rows_i, 0)
    vir_a = lax.dynamic_slice_in_dim(vir_energy, plane * rows_a, rows_a, 0)
    ring = [(z, (z + 1) % planes) for z in range(planes)]

    def step(s, carry):
        block, out = carry
        q = lax.rem(plane - s + planes, planes)
        panel = lax.all_gather(block, "row", axis=1, tiled=True)
        cycle = jnp.einsum("ikac,kcjb->ijab", amplitudes, panel, precision=lax.Precision.HIGHEST)
        occ_j = lax.dynamic_slice_in_dim(occ_energy, q * cols_j, cols_j, 0)
        denom = (
            occ_i[:, None, None, None]
            + occ_j[None, :, None, None]
            - vir_a[None, None, :, None]
            - vir_energy[None, None, None, :]
        )
        out = lax.dynamic_update_slice_in_dim(out, cycle / denom, q * cols_j, 1)
        return lax.ppermute(block, "col", ring), out

    out = jnp.zeros((rows_i, occ_energy.shape[0], rows_a, cols_b), jnp.float32)
    return lax.fori_loop(0, planes, step, (integrals, out))[1]


def split(value):
    high = value.astype(jnp.bfloat16)
    return high, (value - high.astype(jnp.float32)).astype(jnp.bfloat16)


def columns_kernel(pair, core_ref, block, mine, other):
    half = block.shape[2] // 2
    for which in range(2):

        @pl.when(core_ref[0] == which)
        def _(which=which):
            for t in range(2):
                mine[t, 0] = block[0, :, which * half + 2 * pair + t, :]
                other[t, 0] = block[0, :, (1 - which) * half + 2 * pair + t, :]


def columns(integrals, core, pair):
    ks, cs, js, width = integrals.shape
    return pl.pallas_call(
        functools.partial(columns_kernel, pair),
        grid_spec=pltpu.PrefetchScalarGridSpec(
            num_scalar_prefetch=1,
            grid=(ks,),
            in_specs=[pl.BlockSpec((1, cs, js, width), lambda k, _: (k, 0, 0, 0))],
            out_specs=[pl.BlockSpec((2, 1, cs, width), lambda k, _: (0, k, 0, 0))] * 2,
        ),
        out_shape=[jax.ShapeDtypeStruct((2, ks, cs, width), jnp.float32)] * 2,
        compiler_params=pltpu.CompilerParams(vmem_limit_bytes=VMEM),
    )(core.reshape(1), integrals)


def merge_kernel(core_ref, mine, other, out, *room):
    cs = mine.shape[2]
    for source, at in ((mine, core_ref[0]), (other, 1 - core_ref[0])):
        out[0, :, pl.ds(pl.multiple_of(at * cs, cs), cs), :] = source[0]


def merge(mine, other, core, room=None):
    _, ks, cs, width = other.shape
    block = (1, ks, cs, width)
    return pl.pallas_call(
        merge_kernel,
        grid_spec=pltpu.PrefetchScalarGridSpec(
            num_scalar_prefetch=1,
            grid=(2,),
            in_specs=[pl.BlockSpec(block, lambda t, _: (t, 0, 0, 0))] * 2,
            out_specs=[pl.BlockSpec((1, ks, 2 * cs, width), lambda t, _: (t, 0, 0, 0))] + [HBM] * (room is not None),
        ),
        out_shape=[jax.ShapeDtypeStruct((2, ks, 2 * cs, width), jnp.float32)]
        + [jax.ShapeDtypeStruct(r, jnp.float32) for r in [room] if r],
        compiler_params=pltpu.CompilerParams(vmem_limit_bytes=VMEM),
    )(core.reshape(1), mine, other)


def rows_kernel(starts, chip_ref, *refs):
    sources, (high, low) = refs[:-2], refs[-2:]
    step = pl.program_id(0)
    for source, (first, count) in zip(sources, starts):

        @pl.when((step >= first) & (step < first + count))
        def _(source=source):
            ks = source.shape[1]
            n = source.shape[3] // 4
            for m in range(4):
                at = pl.ds(pl.multiple_of((chip_ref[0] ^ m) * n, n), n)
                for k in range(ks):
                    to = pl.ds((m * ks + k) * n, n)
                    high[:, to], low[:, to] = split(source[0, k, :, at])


def rows(values, chip):
    starts, first = [], 0
    for v in values:
        starts.append((first, v.shape[0]))
        first += v.shape[0]
    _, ks, rows_a, depth = values[0].shape
    shape = jax.ShapeDtypeStruct((first * rows_a, ks * depth), jnp.bfloat16)
    return pl.pallas_call(
        functools.partial(rows_kernel, starts),
        grid_spec=pltpu.PrefetchScalarGridSpec(
            num_scalar_prefetch=1,
            grid=(first,),
            in_specs=[
                pl.BlockSpec((1, ks, rows_a, depth), lambda s, _, a=a, n=n: (jnp.clip(s - a, 0, n - 1), 0, 0, 0))
                for a, n in starts
            ],
            out_specs=[pl.BlockSpec((rows_a, ks * depth), lambda s, _: (s, 0))] * 2,
        ),
        out_shape=[shape, shape],
        compiler_params=pltpu.CompilerParams(vmem_limit_bytes=VMEM),
    )(chip.reshape(1), *values)


def each_place(act, gots, blocks, out, keys, at, block, sem):
    for n, got in enumerate(gots):

        @pl.when((keys[at] == 1) & (block < blocks[n]))
        def _(n=n, got=got, at=at):
            copy = pltpu.make_async_copy(got.at[0], out.at[:, keys[at + 1 + block]], sem.at[n])
            getattr(copy, act)()

        at += 1 + blocks[n]


def place_keys(gots):
    return [v for _, js, keep in gots for v in (keep, *js)]


def place_spec(got):
    last = got.shape[0] - 1
    return pl.BlockSpec((1, *got.shape[1:]), lambda b, *_: (jnp.minimum(b, last), 0, 0, 0))


def product_kernel(chunks, starts, blocks, mode, added, keys, occ, a_hi, a_lo, rowd, vir, *refs):
    sets = len(starts) - 1
    pieces, refs = refs[: sets * len(chunks)], refs[sets * len(chunks) :]
    if added:
        start, refs = refs[0], refs[1:]
    places_here = mode == "own" or len(blocks) > 0
    if places_here:
        gots, refs = refs[: len(blocks)], refs[len(blocks) + 1 :]
        out, *refs, got_sem = refs
    if mode == "own":
        send, b_hi, b_lo, own, own_sem = refs
    elif mode == "mine":
        _, own, b_hi, b_lo = refs
    elif mode == "send":
        send, b_hi, b_lo = refs
    elif mode == "lent":
        own, send, b_hi, b_lo = refs
    else:
        part, b_hi, b_lo = refs
    block, step, tiles = pl.program_id(0), pl.program_id(1), pl.num_programs(1)
    own_at, send_at = {"mine": (0, None), "send": (None, 0)}.get(mode, (0, 1))
    ks, n = pieces[0].shape[1:3]
    tile_i = a_hi.shape[0] // 128
    column = keys[1 + block]

    def own_copy():
        return pltpu.make_async_copy(own, out.at[:, column], own_sem.at[0])

    def places(act):
        each_place(act, gots, blocks, out, keys, 1 + starts[-1], block, got_sem)

    if places_here:
        pl.when(step == 0)(lambda: places("start"))

    @pl.when(keys[0] == 1)
    def _():
        for one in range(sets):

            @pl.when((step == 0) & (block >= starts[one]) & (block < starts[one + 1]))
            def _(one=one):
                for m in range(len(chunks)):
                    for k in range(ks):
                        at = pl.ds((m * ks + k) * n, n)
                        b_hi[at, :], b_lo[at, :] = split(pieces[one * len(chunks) + m][0, k])

        cols = slice(0, len(chunks) * ks * n)
        dot = functools.partial(jnp.dot, preferred_element_type=jnp.float32)
        high, low = a_hi[:, cols], a_lo[:, cols]
        value = dot(low, b_hi[...]) + dot(high, b_lo[...]) + dot(high, b_hi[...])
        if added:
            value = value + start[0]
        if mode == "part":
            part[0] = value
        else:
            wide = jnp.concatenate([rowd[...]] * (value.shape[1] // 128), axis=1)
            value = value / (wide + occ[column] - vir[...])
            value = value.reshape(tile_i, 128, value.shape[1])
            if own_at is not None:

                @pl.when(step == own_at)
                def _():
                    if mode == "mine":
                        own[:, 0] = value
                    elif mode == "lent":
                        own[0] = value
                    else:
                        own[...] = value
                        own_copy().start()

            if send_at is not None:

                @pl.when(step == send_at)
                def _():
                    send[0] = value

        if mode == "own":
            pl.when(step == tiles - 1)(lambda: own_copy().wait())

    if places_here:
        pl.when(step == tiles - 1)(lambda: places("wait"))


def product(rows_in, sets, run, js, occ, vir, mode="own", chunks=(0, 1, 2, 3), added=None, added_at=None, out=None, gots=()):
    a_hi, a_lo, rowd = rows_in
    size, whole = a_hi.shape
    _, ks, n, width = sets[0][0].shape
    depth = len(chunks) * ks * n
    starts = [0]
    for pieces in sets:
        starts.append(starts[-1] + pieces[0].shape[0])
    count = starts[-1]
    i_own = size // 256
    tall = size // 2
    first, tiles = {"mine": (0, 1), "send": (1, 1)}.get(mode, (0, 2))
    block = jax.ShapeDtypeStruct((count, i_own, 128, width), jnp.float32)
    block_spec = pl.BlockSpec((1, i_own, 128, width), lambda b, s, *_: (b, 0, 0, 0))
    part_spec = pl.BlockSpec((1, tall, width), lambda b, s, *_: (b, s + first, 0))
    added_at = added_at or (lambda b: b)
    keys = jnp.stack([jnp.asarray(v, jnp.int32) for v in (run, *js, *place_keys(gots))])
    args = [keys, occ, a_hi, a_lo, rowd, vir]
    if chunks[0] == 0:
        a_spec = pl.BlockSpec((tall, whole), lambda b, s, *_: (s + first, 0))
    else:
        a_spec = pl.BlockSpec((tall, depth), lambda b, s, *_: (s + first, chunks[0]))
    specs = [a_spec, a_spec, pl.BlockSpec((tall, 128), lambda b, s, *_: (s + first, 0))]
    specs += [pl.BlockSpec(vir.shape, lambda b, s, *_: (0, 0))]
    for at, pieces in zip(starts, sets):
        last = pieces[0].shape[0] - 1
        args += pieces
        specs += [
            pl.BlockSpec((1, ks, n, width), lambda b, s, *_, at=at, last=last: (jnp.clip(b - at, 0, last), 0, 0, 0))
        ] * len(pieces)
    if added is not None:
        args.append(added)
        specs.append(pl.BlockSpec((1, tall, width), lambda b, s, *_: (added_at(b), s + first, 0)))
    scratch = [pltpu.VMEM((depth, width), jnp.bfloat16)] * 2
    alias = {}
    out_specs, out_shape = [], []
    if mode == "own":
        scratch += [pltpu.VMEM(block.shape[1:], jnp.float32), pltpu.SemaphoreType.DMA((1,))]
    if mode == "mine":
        args.append(out)
        specs.append(HBM)
        alias = {len(args) - 1: 0}
        out_specs = [pl.BlockSpec((i_own, 1, 128, width), lambda b, s, keys, _: (0, keys[1 + b], 0, 0))]
        out_shape = [jax.ShapeDtypeStruct(out.shape, out.dtype)]
    elif mode == "own" or gots:
        args += [*[g for g, _, _ in gots], out]
        specs += [place_spec(g) for g, _, _ in gots] + [HBM]
        alias = {len(args) - 1: 0}
        scratch.append(pltpu.SemaphoreType.DMA((max(len(gots), 1),)))
        out_specs, out_shape = [HBM], [jax.ShapeDtypeStruct(out.shape, out.dtype)]
    if mode in ("own", "send"):
        out_specs, out_shape = out_specs + [block_spec], out_shape + [block]
    elif mode == "lent":
        out_specs, out_shape = [block_spec, block_spec], [block, block]
    elif mode == "part":
        out_specs, out_shape = out_specs + [part_spec], out_shape + [jax.ShapeDtypeStruct((count, size, width), jnp.float32)]
    return pl.pallas_call(
        functools.partial(product_kernel, chunks, starts, [g.shape[0] for g, _, _ in gots], mode, added is not None),
        grid_spec=pltpu.PrefetchScalarGridSpec(
            num_scalar_prefetch=2, grid=(count, tiles), in_specs=specs, out_specs=out_specs, scratch_shapes=scratch
        ),
        out_shape=out_shape,
        input_output_aliases=alias,
        compiler_params=pltpu.CompilerParams(vmem_limit_bytes=VMEM),
        cost_estimate=pl.CostEstimate(
            flops=6 * count * size * depth * width // (2 // tiles),
            bytes_accessed=4 * count * (size * (depth + width) + depth * width),
            transcendentals=0,
        ),
    )(*args)


def place_kernel(blocks, keys, *refs):
    gots, out, sem = refs[: len(blocks)], refs[len(blocks) + 1], refs[len(blocks) + 2]
    for act in ("start", "wait"):
        each_place(act, gots, blocks, out, keys, 0, pl.program_id(0), sem)


def place(out, gots):
    keys = jnp.stack([jnp.asarray(v, jnp.int32) for v in place_keys(gots)])
    blocks = [g.shape[0] for g, _, _ in gots]
    return pl.pallas_call(
        functools.partial(place_kernel, blocks),
        grid_spec=pltpu.PrefetchScalarGridSpec(
            num_scalar_prefetch=1,
            grid=(max(blocks),),
            in_specs=[place_spec(g) for g, _, _ in gots] + [HBM],
            out_specs=HBM,
            scratch_shapes=[pltpu.SemaphoreType.DMA((len(gots),))],
        ),
        out_shape=jax.ShapeDtypeStruct(out.shape, out.dtype),
        input_output_aliases={len(gots) + 1: 0},
        compiler_params=pltpu.CompilerParams(vmem_limit_bytes=VMEM),
    )(keys, *[g for g, _, _ in gots], out)


def finish_kernel(starts, keys, *refs):
    sources, out = refs[: len(starts) - 1], refs[-1]
    for n, source in enumerate(sources):

        @pl.when((pl.program_id(0) >= starts[n]) & (pl.program_id(0) < starts[n + 1]))
        def _(source=source):
            out[:, 0] = source[0]


def finish(out, gots):
    keys = jnp.stack([jnp.asarray(j, jnp.int32) for _, js in gots for j in js])
    starts = [0]
    for got, _ in gots:
        starts.append(starts[-1] + got.shape[0])
    rows_i, _, rows_a, width = out.shape
    return pl.pallas_call(
        functools.partial(finish_kernel, starts),
        grid_spec=pltpu.PrefetchScalarGridSpec(
            num_scalar_prefetch=1,
            grid=(starts[-1],),
            in_specs=[
                pl.BlockSpec((1, *g.shape[1:]), lambda b, _, at=at, n=g.shape[0]: (jnp.clip(b - at, 0, n - 1), 0, 0, 0))
                for at, (g, _) in zip(starts, gots)
            ]
            + [HBM],
            out_specs=pl.BlockSpec((rows_i, 1, rows_a, width), lambda b, keys: (0, keys[b], 0, 0)),
        ),
        out_shape=jax.ShapeDtypeStruct(out.shape, out.dtype),
        input_output_aliases={len(gots) + 1: 0},
        compiler_params=pltpu.CompilerParams(vmem_limit_bytes=VMEM),
    )(keys, *[g for g, _ in gots], out)


def hop(value, mask=0, planes=None, core=0):
    planes = {z: z for z in range(4)} if planes is None else planes
    flip = 2 * mask + core
    pairs = [(r * 4 + z, (r ^ flip) * 4 + w) for r in range(8) for z, w in planes.items()]
    return lax.ppermute(value, AXES, pairs)


def hop_middle(value):
    pairs = [(r * 4 + z, r * 4 + 3 - z) for r in range(8) for z in (1, 2)]
    pairs += [(r * 4 + z, (r ^ 1) * 4 + z) for r in range(8) for z in (0, 3)]
    return lax.ppermute(value, AXES, pairs)


def together(values):
    return lax.optimization_barrier(values)


def body(amplitudes, integrals, occ_energy, vir_energy):
    row, plane = lax.axis_index("row"), lax.axis_index("col")
    core, chip = lax.rem(row, 2), lax.div(row, 2)
    rows_i, ks, rows_a, depth = amplitudes.shape
    cols_j, cols_b = integrals.shape[2:]
    parts = cols_j // 2
    swap = {0: 1, 1: 0, 2: 3, 3: 2}
    is_end = (plane == 0) | (plane == 3)
    is_mid = ~is_end
    vir = vir_energy.reshape(1, -1)

    def share(plane_of):
        occ = [lax.dynamic_slice_in_dim(occ_energy, r * rows_i, rows_i, 0) for r in (row, row ^ 1)]
        part = lax.dynamic_slice_in_dim(vir_energy, plane_of * rows_a, rows_a, 0)
        rowd = (jnp.concatenate(occ)[:, None] - part[None, :]).reshape(-1, 1)
        return jnp.broadcast_to(rowd, (rowd.shape[0], 128))

    def column(w, pair, of_core):
        return (plane ^ w) * cols_j + of_core * parts + 2 * pair

    def either(at_end, at_mid):
        return jnp.where(is_end, at_end, at_mid)

    def along(x, y, z, mid=None, flip=0):
        got = [hop_middle(mid)] if mid is not None else []
        return [hop(x, mask=1), hop(y, mask=2), hop(z, planes=swap, core=flip)] + got

    room = (rows_i, occ_energy.shape[0], rows_a, cols_b)
    mine, other = columns(integrals, core, 0)
    a0, out = merge(mine, hop(other, core=1), core, room)
    state = dict(out=out, gots=[], sends=[])

    def columns_of(w, pair, of_core):
        at = column(w, pair, of_core)
        return [at, at + 1]

    def work(rows_in, sets, where, run=1, **how):
        js = [j for w, pair in where for j in columns_of(w, pair, core)]
        state["out"], send = product(rows_in, sets, run, js, occ_energy, vir, out=state["out"], gots=state["gots"], **how)
        state["gots"] = []
        state["sends"].append((send, [j for w, pair in where for j in columns_of(w, pair, 1 - core)], run))

    def begin(here, sets, where, chunks=(0, 1, 2)):
        js = [j for w, pair in where for j in columns_of(w, pair, core)]
        how = dict(mode="part", chunks=chunks)
        if state["gots"]:
            state["out"], sums = product(
                here, sets, 1, js, occ_energy, vir, out=state["out"], gots=state["gots"], **how
            )
            state["gots"] = []
            return sums
        (sums,) = product(here, sets, 1, js, occ_energy, vir, **how)
        return sums

    def exchange():
        now, state["sends"] = state["sends"], []
        return [(hop(v, core=1), js, keep) for v, js, keep in now]

    def end_round(values, moved=()):
        gots, sends = state["gots"] + list(moved), state["sends"]
        values, new_gots, new_sends, state["out"] = together(
            (values, [g[0] for g in gots], [s[0] for s in sends], state["out"])
        )
        state["gots"] = [(v, *g[1:]) for v, g in zip(new_gots, gots)]
        state["sends"] = [(v, *s[1:]) for v, s in zip(new_sends, sends)]
        return values

    a0x, a0y, a1, a3m = along(a0, a0, a0, a0)
    mine, other = columns(integrals, core, 1)
    (b0,) = merge(mine, hop(other, core=1), core)
    z = either(b0, a3m)
    v = end_round((amplitudes, a0, b0, a0x, a0y, a1, a3m, z))
    amplitudes, a0, b0, a0x, a0y, a1, a3m, z = v
    a_other = hop(amplitudes, core=1)
    a0d, b0y, ab, a2m = along(a0y, b0, z, a1)
    z = either(amplitudes[:2], a2m)
    e3 = either(ab, a2m)
    v = end_round((amplitudes, a_other, a0, b0, a0x, a0y, a0d, a1, a3m, b0y, ab, e3, z))
    amplitudes, a_other, a0, b0, a0x, a0y, a0d, a1, a3m, b0y, ab, e3, z = v
    b0x, e3y, first, b3m = along(b0, e3, z, b0)
    here = (*rows([amplitudes, a_other], chip), share(plane))
    work(here, [(a0, a0x, a0y, a0d)], [(0, 0)])
    z = either(amplitudes[2:], b3m)
    first, state["out"] = together((first, state["out"]))
    first_other = hop(first, core=1)
    v = end_round((here, a0, b0, a0x, a0y, a0d, a1, a3m, b0x, b0y, ab, e3, e3y, first, first_other, b3m, z))
    here, a0, b0, a0x, a0y, a0d, a1, a3m, b0x, b0y, ab, e3, e3y, first, first_other, b3m, z = v
    moved = exchange()
    e3x, b0d, second, b2m = along(e3, b0x, z, ab)
    e6, here = together((either(first, ab), here))
    b_sum = begin(here, [(b0, b0x, b0y)], [(0, 1)])
    z = either(a0x, b2m)
    v = (here, a0, b0, a0x, a0y, a0d, a1, a3m, b0x, b0y, b0d, b2m, b_sum, e3, e3x, e3y, e6, first, first_other, second, b3m, z)
    v = end_round(v, moved)
    here, a0, b0, a0x, a0y, a0d, a1, a3m, b0x, b0y, b0d, b2m, b_sum, e3, e3x, e3y, e6, first, first_other, second, b3m, z = v
    second_other = hop(second, core=1)
    e6x, e6y, third, g3x = along(e6, e6, z, a0x)
    e4, first = together((either(second, b2m), first))
    near = (*rows([first, second, first_other, second_other], chip), share(plane ^ 1))
    s_a, l_a = product(near, [(a0, a0x, a0y, a0d)], is_mid, columns_of(0, 0, core), occ_energy, vir, mode="lent")
    z = either(a0y, s_a)
    v = (here, near, a1, a3m, b0, b0x, b0y, b0d, a0y, a0d, b3m, b_sum, e3, e3x, e3y, e4, e6, e6x, e6y, third, g3x, l_a, z)
    v = end_round(v)
    here, near, a1, a3m, b0, b0x, b0y, b0d, a0y, a0d, b3m, b_sum, e3, e3x, e3y, e4, e6, e6x, e6y, third, g3x, l_a, z = v
    e3d, e6d, fourth, g3y = along(e3y, e6x, z, a0y)
    e5, near = together((either(third, b3m), near))
    s_b, l_b = product(near, [(b0, b0x, b0y, b0d)], is_mid, columns_of(0, 1, core), occ_energy, vir, mode="lent")
    z, here = together((either(a0d, s_b), here))
    work(here, [(b0d,)], [(0, 1)], chunks=(3,), added=b_sum)
    v = (here, a1, a3m, a0d, e3, e3x, e3y, e3d, e4, e5, e6, e6x, e6y, e6d, third, fourth, g3x, g3y, l_a, l_b, z)
    v = end_round(v)
    here, a1, a3m, a0d, e3, e3x, e3y, e3d, e4, e5, e6, e6x, e6y, e6d, third, fourth, g3x, g3y, l_a, l_b, z = v
    state["gots"].append((fourth, columns_of(1, 0, core), is_end))
    moved = exchange()
    e4x, e4y, fifth, g3d = along(e4, e4, z, a0d)
    work(here, [(e3, e3x, e3y, e3d), (e6, e6x, e6y, e6d)], [(2, 0), (either(3, 1), either(0, 1))])
    v = end_round((here, a1, a3m, e4, e4x, e4y, e5, third, fourth, fifth, g3x, g3y, g3d, l_a, l_b), moved)
    here, a1, a3m, e4, e4x, e4y, e5, third, fourth, fifth, g3x, g3y, g3d, l_a, l_b = v
    state["gots"].append((fifth, columns_of(1, 1, core), is_end))
    moved = exchange()
    e5x, e5y, sixth = along(e5, e5, l_a, flip=1)
    work(here, [(a1, third, fourth, fifth), (a3m, g3x, g3y, g3d)], [(1, 0), (3, 0)], is_mid)
    moved.append((sixth, columns_of(1, 0, 1 - core), is_end))
    v = end_round((here, e4, e4x, e4y, e5, e5x, e5y, l_b), moved)
    here, e4, e4x, e4y, e5, e5x, e5y, l_b = v
    moved = exchange()
    e4d, e5d, seventh = along(e4y, e5x, l_b, flip=1)
    last = [(2, 1), (3, 1)]
    js, js_other = ([j for w, pair in last for j in columns_of(w, pair, c)] for c in (core, 1 - core))
    sums = begin(here, [(e4, e4x, e4y), (e5, e5x, e5y)], last)
    sums, state["out"] = together((sums, state["out"]))
    out = place(state["out"], moved)
    here, e4d, e5d, sums, seventh, out = together((here, e4d, e5d, sums, seventh, out))
    how = dict(chunks=(3,), added=sums)
    (send,) = product(here, [(e4d,), (e5d,)], 1, js, occ_energy, vir, mode="send", **how)
    got = hop(send, core=1)
    (out,) = product(here, [(e4d,), (e5d,)], 1, js, occ_energy, vir, mode="mine", out=out, **how)
    js_seventh = [jnp.where(is_end, a, b) for a, b in zip(columns_of(1, 1, 1 - core), js_other)]
    return finish(out, [(seventh, js_seventh), (got, js_other)])


def solution(mesh):
    planned = mesh.shape["row"] == 8 and mesh.shape["col"] == 4
    return jax.shard_map(
        body if planned else streamed,
        mesh=mesh,
        in_specs=(P("row", None, "col", None), P(None, "row", "col", None), P(), P()),
        out_specs=P("row", None, "col", None),
        check_vma=False,
    )
```

```python
import functools

import jax
import jax.numpy as jnp
from jax import lax
from jax.experimental import pallas as pl
from jax.experimental.pallas import tpu as pltpu
from jax.sharding import PartitionSpec as P

AXES = ("row", "col")

HBM = pl.BlockSpec(memory_space=pl.ANY)
VMEM = 44 * 2**20


def streamed(amplitudes, integrals, occ_energy, vir_energy):
    planes = lax.axis_size("col")
    plane = lax.axis_index("col")
    rows_i, _, rows_a, _ = amplitudes.shape
    cols_j, cols_b = integrals.shape[2:]
    occ_i = lax.dynamic_slice_in_dim(occ_energy, lax.axis_index("row") * rows_i, rows_i, 0)
    vir_a = lax.dynamic_slice_in_dim(vir_energy, plane * rows_a, rows_a, 0)
    ring = [(z, (z + 1) % planes) for z in range(planes)]

    def step(s, carry):
        block, out = carry
        q = lax.rem(plane - s + planes, planes)
        panel = lax.all_gather(block, "row", axis=1, tiled=True)
        cycle = jnp.einsum("ikac,kcjb->ijab", amplitudes, panel, precision=lax.Precision.HIGHEST)
        occ_j = lax.dynamic_slice_in_dim(occ_energy, q * cols_j, cols_j, 0)
        denom = (
            occ_i[:, None, None, None]
            + occ_j[None, :, None, None]
            - vir_a[None, None, :, None]
            - vir_energy[None, None, None, :]
        )
        out = lax.dynamic_update_slice_in_dim(out, cycle / denom, q * cols_j, 1)
        return lax.ppermute(block, "col", ring), out

    out = jnp.zeros((rows_i, occ_energy.shape[0], rows_a, cols_b), jnp.float32)
    return lax.fori_loop(0, planes, step, (integrals, out))[1]


def split(value):
    high = value.astype(jnp.bfloat16)
    return high, (value - high.astype(jnp.float32)).astype(jnp.bfloat16)


def columns_kernel(pair, core_ref, block, mine, other):
    half = block.shape[2] // 2
    for which in range(2):

        @pl.when(core_ref[0] == which)
        def _(which=which):
            for t in range(2):
                mine[t, 0] = block[0, :, which * half + 2 * pair + t, :]
                other[t, 0] = block[0, :, (1 - which) * half + 2 * pair + t, :]


def columns(integrals, core, pair):
    ks, cs, js, width = integrals.shape
    return pl.pallas_call(
        functools.partial(columns_kernel, pair),
        grid_spec=pltpu.PrefetchScalarGridSpec(
            num_scalar_prefetch=1,
            grid=(ks,),
            in_specs=[pl.BlockSpec((1, cs, js, width), lambda k, _: (k, 0, 0, 0))],
            out_specs=[pl.BlockSpec((2, 1, cs, width), lambda k, _: (0, k, 0, 0))] * 2,
        ),
        out_shape=[jax.ShapeDtypeStruct((2, ks, cs, width), jnp.float32)] * 2,
        compiler_params=pltpu.CompilerParams(vmem_limit_bytes=VMEM // 2),
    )(core.reshape(1), integrals)


def merge_kernel(core_ref, mine, other, out, *room):
    cs = mine.shape[2]
    for source, at in ((mine, core_ref[0]), (other, 1 - core_ref[0])):
        out[0, :, pl.ds(pl.multiple_of(at * cs, cs), cs), :] = source[0]


def merge(mine, other, core, room=None):
    _, ks, cs, width = other.shape
    block = (1, ks, cs, width)
    return pl.pallas_call(
        merge_kernel,
        grid_spec=pltpu.PrefetchScalarGridSpec(
            num_scalar_prefetch=1,
            grid=(2,),
            in_specs=[pl.BlockSpec(block, lambda t, _: (t, 0, 0, 0))] * 2,
            out_specs=[pl.BlockSpec((1, ks, 2 * cs, width), lambda t, _: (t, 0, 0, 0))] + [HBM] * (room is not None),
        ),
        out_shape=[jax.ShapeDtypeStruct((2, ks, 2 * cs, width), jnp.float32)]
        + [jax.ShapeDtypeStruct(r, jnp.float32) for r in [room] if r],
        compiler_params=pltpu.CompilerParams(vmem_limit_bytes=VMEM // 2),
    )(core.reshape(1), mine, other)


def rows_kernel(starts, chip_ref, *refs):
    sources, (high, low) = refs[:-2], refs[-2:]
    step = pl.program_id(0)
    for source, (first, count) in zip(sources, starts):

        @pl.when((step >= first) & (step < first + count))
        def _(source=source):
            ks = source.shape[1]
            n = source.shape[3] // 4
            for m in range(4):
                at = pl.ds(pl.multiple_of((chip_ref[0] ^ m) * n, n), n)
                for k in range(ks):
                    to = pl.ds((m * ks + k) * n, n)
                    high[:, to], low[:, to] = split(source[0, k, :, at])


def rows(values, chip):
    starts, first = [], 0
    for v in values:
        starts.append((first, v.shape[0]))
        first += v.shape[0]
    _, ks, rows_a, depth = values[0].shape
    shape = jax.ShapeDtypeStruct((first * rows_a, ks * depth), jnp.bfloat16)
    return pl.pallas_call(
        functools.partial(rows_kernel, starts),
        grid_spec=pltpu.PrefetchScalarGridSpec(
            num_scalar_prefetch=1,
            grid=(first,),
            in_specs=[
                pl.BlockSpec((1, ks, rows_a, depth), lambda s, _, a=a, n=n: (jnp.clip(s - a, 0, n - 1), 0, 0, 0))
                for a, n in starts
            ],
            out_specs=[pl.BlockSpec((rows_a, ks * depth), lambda s, _: (s, 0))] * 2,
        ),
        out_shape=[shape, shape],
        compiler_params=pltpu.CompilerParams(vmem_limit_bytes=VMEM // 2),
    )(chip.reshape(1), *values)


def each_place(act, gots, blocks, out, keys, at, block, sem):
    for n, got in enumerate(gots):

        @pl.when((keys[at] == 1) & (block < blocks[n]))
        def _(n=n, got=got, at=at):
            copy = pltpu.make_async_copy(got.at[0], out.at[:, keys[at + 1 + block]], sem.at[n])
            getattr(copy, act)()

        at += 1 + blocks[n]


def place_keys(gots):
    return [v for _, js, keep in gots for v in (keep, *js)]


def place_spec(got):
    last = got.shape[0] - 1
    return pl.BlockSpec((1, *got.shape[1:]), lambda b, *_: (jnp.minimum(b, last), 0, 0, 0))


def product_kernel(chunks, starts, blocks, mode, added, keys, occ, a_hi, a_lo, rowd, vir, *refs):
    sets = len(starts) - 1
    pieces, refs = refs[: sets * len(chunks)], refs[sets * len(chunks) :]
    if added:
        start, refs = refs[0], refs[1:]
    places_here = mode == "own" or len(blocks) > 0
    if places_here:
        gots, refs = refs[: len(blocks)], refs[len(blocks) + 1 :]
        out, *refs, got_sem = refs
    if mode == "own":
        send, b_hi, b_lo, own, own_sem = refs
    elif mode == "mine":
        _, own, b_hi, b_lo = refs
    elif mode == "send":
        send, b_hi, b_lo = refs
    elif mode == "lent":
        own, send, b_hi, b_lo = refs
    else:
        part, b_hi, b_lo = refs
    block, step, tiles = pl.program_id(0), pl.program_id(1), pl.num_programs(1)
    own_at, send_at = {"mine": (0, None), "send": (None, 0)}.get(mode, (0, 1))
    ks, n = pieces[0].shape[1:3]
    tile_i = a_hi.shape[0] // 128
    column = keys[1 + block]

    def own_copy():
        return pltpu.make_async_copy(own, out.at[:, column], own_sem.at[0])

    def places(act):
        each_place(act, gots, blocks, out, keys, 1 + starts[-1], block, got_sem)

    if places_here:
        pl.when(step == 0)(lambda: places("start"))

    @pl.when(keys[0] == 1)
    def _():
        for one in range(sets):

            @pl.when((step == 0) & (block >= starts[one]) & (block < starts[one + 1]))
            def _(one=one):
                for m in range(len(chunks)):
                    for k in range(ks):
                        at = pl.ds((m * ks + k) * n, n)
                        b_hi[at, :], b_lo[at, :] = split(pieces[one * len(chunks) + m][0, k])

        cols = slice(0, len(chunks) * ks * n)
        dot = functools.partial(jnp.dot, preferred_element_type=jnp.float32)
        high, low = a_hi[:, cols], a_lo[:, cols]
        value = dot(low, b_hi[...]) + dot(high, b_lo[...]) + dot(high, b_hi[...])
        if added:
            value = value + start[0]
        if mode == "part":
            part[0] = value
        else:
            wide = jnp.concatenate([rowd[...]] * (value.shape[1] // 128), axis=1)
            value = value / (wide + occ[column] - vir[...])
            value = value.reshape(tile_i, 128, value.shape[1])
            if own_at is not None:

                @pl.when(step == own_at)
                def _():
                    if mode == "mine":
                        own[:, 0] = value
                    elif mode == "lent":
                        own[0] = value
                    else:
                        own[...] = value
                        own_copy().start()

            if send_at is not None:

                @pl.when(step == send_at)
                def _():
                    send[0] = value

        if mode == "own":
            pl.when(step == tiles - 1)(lambda: own_copy().wait())

    if places_here:
        pl.when(step == tiles - 1)(lambda: places("wait"))


def product(rows_in, sets, run, js, occ, vir, mode="own", chunks=(0, 1, 2, 3), added=None, added_at=None, out=None, gots=()):
    a_hi, a_lo, rowd = rows_in
    size, whole = a_hi.shape
    _, ks, n, width = sets[0][0].shape
    depth = len(chunks) * ks * n
    starts = [0]
    for pieces in sets:
        starts.append(starts[-1] + pieces[0].shape[0])
    count = starts[-1]
    i_own = size // 256
    tall = size // 2
    first, tiles = {"mine": (0, 1), "send": (1, 1)}.get(mode, (0, 2))
    block = jax.ShapeDtypeStruct((count, i_own, 128, width), jnp.float32)
    block_spec = pl.BlockSpec((1, i_own, 128, width), lambda b, s, *_: (b, 0, 0, 0))
    part_spec = pl.BlockSpec((1, tall, width), lambda b, s, *_: (b, s + first, 0))
    added_at = added_at or (lambda b: b)
    keys = jnp.stack([jnp.asarray(v, jnp.int32) for v in (run, *js, *place_keys(gots))])
    args = [keys, occ, a_hi, a_lo, rowd, vir]
    if chunks[0] == 0:
        a_spec = pl.BlockSpec((tall, whole), lambda b, s, *_: (s + first, 0))
    else:
        a_spec = pl.BlockSpec((tall, depth), lambda b, s, *_: (s + first, chunks[0]))
    specs = [a_spec, a_spec, pl.BlockSpec((tall, 128), lambda b, s, *_: (s + first, 0))]
    specs += [pl.BlockSpec(vir.shape, lambda b, s, *_: (0, 0))]
    for at, pieces in zip(starts, sets):
        last = pieces[0].shape[0] - 1
        args += pieces
        specs += [
            pl.BlockSpec((1, ks, n, width), lambda b, s, *_, at=at, last=last: (jnp.clip(b - at, 0, last), 0, 0, 0))
        ] * len(pieces)
    if added is not None:
        args.append(added)
        specs.append(pl.BlockSpec((1, tall, width), lambda b, s, *_: (added_at(b), s + first, 0)))
    scratch = [pltpu.VMEM((depth, width), jnp.bfloat16)] * 2
    alias = {}
    out_specs, out_shape = [], []
    if mode == "own":
        scratch += [pltpu.VMEM(block.shape[1:], jnp.float32), pltpu.SemaphoreType.DMA((1,))]
    if mode == "mine":
        args.append(out)
        specs.append(HBM)
        alias = {len(args) - 1: 0}
        out_specs = [pl.BlockSpec((i_own, 1, 128, width), lambda b, s, keys, _: (0, keys[1 + b], 0, 0))]
        out_shape = [jax.ShapeDtypeStruct(out.shape, out.dtype)]
    elif mode == "own" or gots:
        args += [*[g for g, _, _ in gots], out]
        specs += [place_spec(g) for g, _, _ in gots] + [HBM]
        alias = {len(args) - 1: 0}
        scratch.append(pltpu.SemaphoreType.DMA((max(len(gots), 1),)))
        out_specs, out_shape = [HBM], [jax.ShapeDtypeStruct(out.shape, out.dtype)]
    if mode in ("own", "send"):
        out_specs, out_shape = out_specs + [block_spec], out_shape + [block]
    elif mode == "lent":
        out_specs, out_shape = [block_spec, block_spec], [block, block]
    elif mode == "part":
        out_specs, out_shape = out_specs + [part_spec], out_shape + [jax.ShapeDtypeStruct((count, size, width), jnp.float32)]
    return pl.pallas_call(
        functools.partial(product_kernel, chunks, starts, [g.shape[0] for g, _, _ in gots], mode, added is not None),
        grid_spec=pltpu.PrefetchScalarGridSpec(
            num_scalar_prefetch=2, grid=(count, tiles), in_specs=specs, out_specs=out_specs, scratch_shapes=scratch
        ),
        out_shape=out_shape,
        input_output_aliases=alias,
        compiler_params=pltpu.CompilerParams(vmem_limit_bytes=VMEM if len(sets) > 1 else 3 * VMEM // 4),
        cost_estimate=pl.CostEstimate(
            flops=6 * count * size * depth * width // (2 // tiles),
            bytes_accessed=4 * count * (size * (depth + width) + depth * width),
            transcendentals=0,
        ),
    )(*args)


def place_kernel(blocks, keys, *refs):
    gots, out, sem = refs[: len(blocks)], refs[len(blocks) + 1], refs[len(blocks) + 2]
    for act in ("start", "wait"):
        each_place(act, gots, blocks, out, keys, 0, pl.program_id(0), sem)


def place(out, gots):
    keys = jnp.stack([jnp.asarray(v, jnp.int32) for v in place_keys(gots)])
    blocks = [g.shape[0] for g, _, _ in gots]
    return pl.pallas_call(
        functools.partial(place_kernel, blocks),
        grid_spec=pltpu.PrefetchScalarGridSpec(
            num_scalar_prefetch=1,
            grid=(max(blocks),),
            in_specs=[place_spec(g) for g, _, _ in gots] + [HBM],
            out_specs=HBM,
            scratch_shapes=[pltpu.SemaphoreType.DMA((len(gots),))],
        ),
        out_shape=jax.ShapeDtypeStruct(out.shape, out.dtype),
        input_output_aliases={len(gots) + 1: 0},
        compiler_params=pltpu.CompilerParams(vmem_limit_bytes=VMEM // 2),
    )(keys, *[g for g, _, _ in gots], out)


def finish_kernel(keys, got, _, out):
    out[:, 0] = got[0]


def finish(out, got, js):
    rows_i, _, rows_a, width = out.shape
    return pl.pallas_call(
        finish_kernel,
        grid_spec=pltpu.PrefetchScalarGridSpec(
            num_scalar_prefetch=1,
            grid=(got.shape[0],),
            in_specs=[pl.BlockSpec((1, *got.shape[1:]), lambda b, _: (b, 0, 0, 0)), HBM],
            out_specs=pl.BlockSpec((rows_i, 1, rows_a, width), lambda b, keys: (0, keys[b], 0, 0)),
        ),
        out_shape=jax.ShapeDtypeStruct(out.shape, out.dtype),
        input_output_aliases={2: 0},
        compiler_params=pltpu.CompilerParams(vmem_limit_bytes=VMEM // 2),
    )(jnp.stack(js), got, out)


def hop(value, mask=0, planes=None, core=0):
    planes = {z: z for z in range(4)} if planes is None else planes
    flip = 2 * mask + core
    pairs = [(r * 4 + z, (r ^ flip) * 4 + w) for r in range(8) for z, w in planes.items()]
    return lax.ppermute(value, AXES, pairs)


def hop_middle(value):
    pairs = [(r * 4 + z, r * 4 + 3 - z) for r in range(8) for z in (1, 2)]
    pairs += [(r * 4 + z, (r ^ 1) * 4 + z) for r in range(8) for z in (0, 3)]
    return lax.ppermute(value, AXES, pairs)


def together(values):
    return lax.optimization_barrier(values)


def body(amplitudes, integrals, occ_energy, vir_energy):
    row, plane = lax.axis_index("row"), lax.axis_index("col")
    core, chip = lax.rem(row, 2), lax.div(row, 2)
    rows_i, ks, rows_a, depth = amplitudes.shape
    cols_j, cols_b = integrals.shape[2:]
    parts = cols_j // 2
    swap = {0: 1, 1: 0, 2: 3, 3: 2}
    is_end = (plane == 0) | (plane == 3)
    is_mid = ~is_end
    vir = vir_energy.reshape(1, -1)

    def share(plane_of):
        occ = [lax.dynamic_slice_in_dim(occ_energy, r * rows_i, rows_i, 0) for r in (row, row ^ 1)]
        part = lax.dynamic_slice_in_dim(vir_energy, plane_of * rows_a, rows_a, 0)
        rowd = (jnp.concatenate(occ)[:, None] - part[None, :]).reshape(-1, 1)
        return jnp.broadcast_to(rowd, (rowd.shape[0], 128))

    def column(w, pair, of_core):
        return (plane ^ w) * cols_j + of_core * parts + 2 * pair

    def either(at_end, at_mid):
        return jnp.where(is_end, at_end, at_mid)

    def along(x, y, z, mid=None, flip=0):
        got = [hop_middle(mid)] if mid is not None else []
        return [hop(x, mask=1), hop(y, mask=2), hop(z, planes=swap, core=flip)] + got

    room = (rows_i, occ_energy.shape[0], rows_a, cols_b)
    mine, other = columns(integrals, core, 0)
    a0, out = merge(mine, hop(other, core=1), core, room)
    state = dict(out=out, gots=[], sends=[])

    def columns_of(w, pair, of_core):
        at = column(w, pair, of_core)
        return [at, at + 1]

    def work(rows_in, sets, where, run=1, **how):
        js = [j for w, pair in where for j in columns_of(w, pair, core)]
        state["out"], send = product(rows_in, sets, run, js, occ_energy, vir, out=state["out"], gots=state["gots"], **how)
        state["gots"] = []
        state["sends"].append((send, [j for w, pair in where for j in columns_of(w, pair, 1 - core)], run))

    def begin(here, sets, where, chunks=(0, 1, 2)):
        js = [j for w, pair in where for j in columns_of(w, pair, core)]
        how = dict(mode="part", chunks=chunks)
        if state["gots"]:
            state["out"], sums = product(
                here, sets, 1, js, occ_energy, vir, out=state["out"], gots=state["gots"], **how
            )
            state["gots"] = []
            return sums
        (sums,) = product(here, sets, 1, js, occ_energy, vir, **how)
        return sums

    def exchange():
        now, state["sends"] = state["sends"], []
        return [(hop(v, core=1), js, keep) for v, js, keep in now]

    def end_round(values, moved=()):
        gots, sends = state["gots"] + list(moved), state["sends"]
        values, new_gots, new_sends, state["out"] = together(
            (values, [g[0] for g in gots], [s[0] for s in sends], state["out"])
        )
        state["gots"] = [(v, *g[1:]) for v, g in zip(new_gots, gots)]
        state["sends"] = [(v, *s[1:]) for v, s in zip(new_sends, sends)]
        return values

    a0x, a0y, a1, a3m = along(a0, a0, a0, a0)
    mine, other = columns(integrals, core, 1)
    (b0,) = merge(mine, hop(other, core=1), core)
    z = either(b0, a3m)
    v = end_round((amplitudes, a0, b0, a0x, a0y, a1, a3m, z))
    amplitudes, a0, b0, a0x, a0y, a1, a3m, z = v
    a_other = hop(amplitudes, core=1)
    a0d, b0y, ab, a2m = along(a0y, b0, z, a1)
    z = either(amplitudes[:2], a2m)
    e3 = either(ab, a2m)
    v = end_round((amplitudes, a_other, a0, b0, a0x, a0y, a0d, a1, a3m, b0y, ab, e3, z))
    amplitudes, a_other, a0, b0, a0x, a0y, a0d, a1, a3m, b0y, ab, e3, z = v
    b0x, e3y, first, b3m = along(b0, e3, z, b0)
    here = (*rows([amplitudes, a_other], chip), share(plane))
    work(here, [(a0, a0x, a0y, a0d)], [(0, 0)])
    z = either(amplitudes[2:], b3m)
    first, state["out"] = together((first, state["out"]))
    first_other = hop(first, core=1)
    v = end_round((here, a0, b0, a0x, a0y, a0d, a1, a3m, b0x, b0y, ab, e3, e3y, first, first_other, b3m, z))
    here, a0, b0, a0x, a0y, a0d, a1, a3m, b0x, b0y, ab, e3, e3y, first, first_other, b3m, z = v
    moved = exchange()
    e3x, b0d, second, b2m = along(e3, b0x, z, ab)
    e6, here = together((either(first, ab), here))
    b_sum = begin(here, [(b0, b0x, b0y)], [(0, 1)])
    z = either(a0x, b2m)
    v = (here, a0, b0, a0x, a0y, a0d, a1, a3m, b0x, b0y, b0d, b2m, b_sum, e3, e3x, e3y, e6, first, first_other, second, b3m, z)
    v = end_round(v, moved)
    here, a0, b0, a0x, a0y, a0d, a1, a3m, b0x, b0y, b0d, b2m, b_sum, e3, e3x, e3y, e6, first, first_other, second, b3m, z = v
    second_other = hop(second, core=1)
    e6x, e6y, third, g3x = along(e6, e6, z, a0x)
    e4, first = together((either(second, b2m), first))
    near = (*rows([first, second, first_other, second_other], chip), share(plane ^ 1))
    s_a, l_a = product(near, [(a0, a0x, a0y, a0d)], is_mid, columns_of(0, 0, core), occ_energy, vir, mode="lent")
    z = either(a0y, s_a)
    v = (here, near, a1, a3m, b0, b0x, b0y, b0d, a0y, a0d, b3m, b_sum, e3, e3x, e3y, e4, e6, e6x, e6y, third, g3x, l_a, z)
    v = end_round(v)
    here, near, a1, a3m, b0, b0x, b0y, b0d, a0y, a0d, b3m, b_sum, e3, e3x, e3y, e4, e6, e6x, e6y, third, g3x, l_a, z = v
    e3d, e6d, fourth, g3y = along(e3y, e6x, z, a0y)
    e5, near = together((either(third, b3m), near))
    s_b, l_b = product(near, [(b0, b0x, b0y, b0d)], is_mid, columns_of(0, 1, core), occ_energy, vir, mode="lent")
    z, here = together((either(a0d, s_b), here))
    work(here, [(b0d,)], [(0, 1)], chunks=(3,), added=b_sum)
    v = (here, a1, a3m, a0d, e3, e3x, e3y, e3d, e4, e5, e6, e6x, e6y, e6d, third, fourth, g3x, g3y, l_a, l_b, z)
    v = end_round(v)
    here, a1, a3m, a0d, e3, e3x, e3y, e3d, e4, e5, e6, e6x, e6y, e6d, third, fourth, g3x, g3y, l_a, l_b, z = v
    state["gots"].append((fourth, columns_of(1, 0, core), is_end))
    moved = exchange()
    e4x, e4y, fifth, g3d = along(e4, e4, z, a0d)
    work(here, [(e3, e3x, e3y, e3d), (e6, e6x, e6y, e6d)], [(2, 0), (either(3, 1), either(0, 1))])
    v = end_round((here, a1, a3m, e4, e4x, e4y, e5, third, fourth, fifth, g3x, g3y, g3d, l_a, l_b), moved)
    here, a1, a3m, e4, e4x, e4y, e5, third, fourth, fifth, g3x, g3y, g3d, l_a, l_b = v
    state["gots"].append((fifth, columns_of(1, 1, core), is_end))
    moved = exchange()
    e5x, e5y, sixth = along(e5, e5, l_a, flip=1)
    work(here, [(a1, third, fourth, fifth), (a3m, g3x, g3y, g3d)], [(1, 0), (3, 0)], is_mid)
    moved.append((sixth, columns_of(1, 0, 1 - core), is_end))
    v = end_round((here, e4, e4x, e4y, e5, e5x, e5y, l_b), moved)
    here, e4, e4x, e4y, e5, e5x, e5y, l_b = v
    moved = exchange()
    e4d, e5d, seventh = along(e4y, e5x, l_b, flip=1)
    last = [(2, 1), (3, 1)]
    js, js_other = ([j for w, pair in last for j in columns_of(w, pair, c)] for c in (core, 1 - core))
    sums = begin(here, [(e4, e4x, e4y), (e5, e5x, e5y)], last)
    sums, state["out"] = together((sums, state["out"]))
    out = place(state["out"], moved)
    here, e4d, e5d, sums, seventh, out = together((here, e4d, e5d, sums, seventh, out))
    how = dict(chunks=(3,), added=sums)
    gots = [(seventh, columns_of(1, 1, 1 - core), is_end)]
    out, send = product(here, [(e4d,), (e5d,)], 1, js, occ_energy, vir, mode="send", out=out, gots=gots, **how)
    got = hop(send, core=1)
    (out,) = product(here, [(e4d,), (e5d,)], 1, js, occ_energy, vir, mode="mine", out=out, **how)
    return finish(out, got, js_other)


def solution(mesh):
    planned = mesh.shape["row"] == 8 and mesh.shape["col"] == 4
    return jax.shard_map(
        body if planned else streamed,
        mesh=mesh,
        in_specs=(P("row", None, "col", None), P(None, "row", "col", None), P(), P()),
        out_specs=P("row", None, "col", None),
        check_vma=False,
    )
```

```python
import functools

import jax
import jax.numpy as jnp
from jax import lax
from jax.experimental import pallas as pl
from jax.experimental.pallas import tpu as pltpu
from jax.sharding import PartitionSpec as P

AXES = ("row", "col")

HBM = pl.BlockSpec(memory_space=pl.ANY)
VMEM = 44 * 2**20


def streamed(amplitudes, integrals, occ_energy, vir_energy):
    planes = lax.axis_size("col")
    plane = lax.axis_index("col")
    rows_i, _, rows_a, _ = amplitudes.shape
    cols_j, cols_b = integrals.shape[2:]
    occ_i = lax.dynamic_slice_in_dim(occ_energy, lax.axis_index("row") * rows_i, rows_i, 0)
    vir_a = lax.dynamic_slice_in_dim(vir_energy, plane * rows_a, rows_a, 0)
    ring = [(z, (z + 1) % planes) for z in range(planes)]

    def step(s, carry):
        block, out = carry
        q = lax.rem(plane - s + planes, planes)
        panel = lax.all_gather(block, "row", axis=1, tiled=True)
        cycle = jnp.einsum("ikac,kcjb->ijab", amplitudes, panel, precision=lax.Precision.HIGHEST)
        occ_j = lax.dynamic_slice_in_dim(occ_energy, q * cols_j, cols_j, 0)
        denom = (
            occ_i[:, None, None, None]
            + occ_j[None, :, None, None]
            - vir_a[None, None, :, None]
            - vir_energy[None, None, None, :]
        )
        out = lax.dynamic_update_slice_in_dim(out, cycle / denom, q * cols_j, 1)
        return lax.ppermute(block, "col", ring), out

    out = jnp.zeros((rows_i, occ_energy.shape[0], rows_a, cols_b), jnp.float32)
    return lax.fori_loop(0, planes, step, (integrals, out))[1]


def split(value):
    high = value.astype(jnp.bfloat16)
    return high, (value - high.astype(jnp.float32)).astype(jnp.bfloat16)


def columns_kernel(pair, core_ref, block, mine, other):
    half = block.shape[2] // 2
    for which in range(2):

        @pl.when(core_ref[0] == which)
        def _(which=which):
            for t in range(2):
                mine[t, 0] = block[0, :, which * half + 2 * pair + t, :]
                other[t, 0] = block[0, :, (1 - which) * half + 2 * pair + t, :]


def columns(integrals, core, pair):
    ks, cs, js, width = integrals.shape
    return pl.pallas_call(
        functools.partial(columns_kernel, pair),
        grid_spec=pltpu.PrefetchScalarGridSpec(
            num_scalar_prefetch=1,
            grid=(ks,),
            in_specs=[pl.BlockSpec((1, cs, js, width), lambda k, _: (k, 0, 0, 0))],
            out_specs=[pl.BlockSpec((2, 1, cs, width), lambda k, _: (0, k, 0, 0))] * 2,
        ),
        out_shape=[jax.ShapeDtypeStruct((2, ks, cs, width), jnp.float32)] * 2,
        compiler_params=pltpu.CompilerParams(vmem_limit_bytes=VMEM // 2),
    )(core.reshape(1), integrals)


def merge_kernel(core_ref, mine, other, out, *room):
    cs = mine.shape[2]
    for source, at in ((mine, core_ref[0]), (other, 1 - core_ref[0])):
        out[0, :, pl.ds(pl.multiple_of(at * cs, cs), cs), :] = source[0]


def merge(mine, other, core, room=None):
    _, ks, cs, width = other.shape
    block = (1, ks, cs, width)
    return pl.pallas_call(
        merge_kernel,
        grid_spec=pltpu.PrefetchScalarGridSpec(
            num_scalar_prefetch=1,
            grid=(2,),
            in_specs=[pl.BlockSpec(block, lambda t, _: (t, 0, 0, 0))] * 2,
            out_specs=[pl.BlockSpec((1, ks, 2 * cs, width), lambda t, _: (t, 0, 0, 0))] + [HBM] * (room is not None),
        ),
        out_shape=[jax.ShapeDtypeStruct((2, ks, 2 * cs, width), jnp.float32)]
        + [jax.ShapeDtypeStruct(r, jnp.float32) for r in [room] if r],
        compiler_params=pltpu.CompilerParams(vmem_limit_bytes=VMEM // 2),
    )(core.reshape(1), mine, other)


def rows_kernel(starts, chip_ref, *refs):
    sources, (high, low) = refs[:-2], refs[-2:]
    step = pl.program_id(0)
    for source, (first, count) in zip(sources, starts):

        @pl.when((step >= first) & (step < first + count))
        def _(source=source):
            ks = source.shape[1]
            n = source.shape[3] // 4
            for m in range(4):
                at = pl.ds(pl.multiple_of((chip_ref[0] ^ m) * n, n), n)
                for k in range(ks):
                    to = pl.ds((m * ks + k) * n, n)
                    high[:, to], low[:, to] = split(source[0, k, :, at])


def rows(values, chip):
    starts, first = [], 0
    for v in values:
        starts.append((first, v.shape[0]))
        first += v.shape[0]
    _, ks, rows_a, depth = values[0].shape
    shape = jax.ShapeDtypeStruct((first * rows_a, ks * depth), jnp.bfloat16)
    return pl.pallas_call(
        functools.partial(rows_kernel, starts),
        grid_spec=pltpu.PrefetchScalarGridSpec(
            num_scalar_prefetch=1,
            grid=(first,),
            in_specs=[
                pl.BlockSpec((1, ks, rows_a, depth), lambda s, _, a=a, n=n: (jnp.clip(s - a, 0, n - 1), 0, 0, 0))
                for a, n in starts
            ],
            out_specs=[pl.BlockSpec((rows_a, ks * depth), lambda s, _: (s, 0))] * 2,
        ),
        out_shape=[shape, shape],
        compiler_params=pltpu.CompilerParams(vmem_limit_bytes=VMEM // 2),
    )(chip.reshape(1), *values)


def each_place(act, gots, blocks, out, keys, at, block, sem):
    for n, got in enumerate(gots):

        @pl.when((keys[at] == 1) & (block < blocks[n]))
        def _(n=n, got=got, at=at):
            copy = pltpu.make_async_copy(got.at[0], out.at[:, keys[at + 1 + block]], sem.at[n])
            getattr(copy, act)()

        at += 1 + blocks[n]


def place_keys(gots):
    return [v for _, js, keep in gots for v in (keep, *js)]


def place_spec(got):
    last = got.shape[0] - 1
    return pl.BlockSpec((1, *got.shape[1:]), lambda b, *_: (jnp.minimum(b, last), 0, 0, 0))


def product_kernel(chunks, starts, blocks, mode, added, keys, occ, a_hi, a_lo, rowd, vir, *refs):
    sets = len(starts) - 1
    pieces, refs = refs[: sets * len(chunks)], refs[sets * len(chunks) :]
    if added:
        start, refs = refs[0], refs[1:]
    places_here = mode == "own" or len(blocks) > 0
    if places_here:
        gots, refs = refs[: len(blocks)], refs[len(blocks) + 1 :]
        out, *refs, got_sem = refs
    if mode == "own":
        send, b_hi, b_lo, own, own_sem = refs
    elif mode == "mine":
        _, own, b_hi, b_lo = refs
    elif mode == "send":
        send, b_hi, b_lo = refs
    elif mode == "lent":
        own, send, b_hi, b_lo = refs
    else:
        part, b_hi, b_lo = refs
    block, step, tiles = pl.program_id(0), pl.program_id(1), pl.num_programs(1)
    own_at, send_at = {"mine": (0, None), "send": (None, 0)}.get(mode, (0, 1))
    ks, n = pieces[0].shape[1:3]
    tile_i = a_hi.shape[0] // 128
    column = keys[1 + block]

    def own_copy():
        return pltpu.make_async_copy(own, out.at[:, column], own_sem.at[0])

    def places(act):
        each_place(act, gots, blocks, out, keys, 1 + starts[-1], block, got_sem)

    if places_here:
        pl.when(step == 0)(lambda: places("start"))

    @pl.when(keys[0] == 1)
    def _():
        for one in range(sets):

            @pl.when((step == 0) & (block >= starts[one]) & (block < starts[one + 1]))
            def _(one=one):
                for m in range(len(chunks)):
                    for k in range(ks):
                        at = pl.ds((m * ks + k) * n, n)
                        b_hi[at, :], b_lo[at, :] = split(pieces[one * len(chunks) + m][0, k])

        cols = slice(0, len(chunks) * ks * n)
        dot = functools.partial(jnp.dot, preferred_element_type=jnp.float32)
        high, low = a_hi[:, cols], a_lo[:, cols]
        value = dot(low, b_hi[...]) + dot(high, b_lo[...]) + dot(high, b_hi[...])
        if added:
            value = value + start[0]
        if mode == "part":
            part[0] = value
        else:
            wide = jnp.concatenate([rowd[...]] * (value.shape[1] // 128), axis=1)
            value = value / (wide + occ[column] - vir[...])
            value = value.reshape(tile_i, 128, value.shape[1])
            if own_at is not None:

                @pl.when(step == own_at)
                def _():
                    if mode == "mine":
                        own[:, 0] = value
                    elif mode == "lent":
                        own[0] = value
                    else:
                        own[...] = value
                        own_copy().start()

            if send_at is not None:

                @pl.when(step == send_at)
                def _():
                    send[0] = value

        if mode == "own":
            pl.when(step == tiles - 1)(lambda: own_copy().wait())

    if places_here:
        pl.when(step == tiles - 1)(lambda: places("wait"))


def product(rows_in, sets, run, js, occ, vir, mode="own", chunks=(0, 1, 2, 3), added=None, added_at=None, out=None, gots=()):
    a_hi, a_lo, rowd = rows_in
    size, whole = a_hi.shape
    _, ks, n, width = sets[0][0].shape
    depth = len(chunks) * ks * n
    starts = [0]
    for pieces in sets:
        starts.append(starts[-1] + pieces[0].shape[0])
    count = starts[-1]
    i_own = size // 256
    tall = size // 2
    first, tiles = {"mine": (0, 1), "send": (1, 1)}.get(mode, (0, 2))
    block = jax.ShapeDtypeStruct((count, i_own, 128, width), jnp.float32)
    block_spec = pl.BlockSpec((1, i_own, 128, width), lambda b, s, *_: (b, 0, 0, 0))
    part_spec = pl.BlockSpec((1, tall, width), lambda b, s, *_: (b, s + first, 0))
    added_at = added_at or (lambda b: b)
    keys = jnp.stack([jnp.asarray(v, jnp.int32) for v in (run, *js, *place_keys(gots))])
    args = [keys, occ, a_hi, a_lo, rowd, vir]
    if chunks[0] == 0:
        a_spec = pl.BlockSpec((tall, whole), lambda b, s, *_: (s + first, 0))
    else:
        a_spec = pl.BlockSpec((tall, depth), lambda b, s, *_: (s + first, chunks[0]))
    specs = [a_spec, a_spec, pl.BlockSpec((tall, 128), lambda b, s, *_: (s + first, 0))]
    specs += [pl.BlockSpec(vir.shape, lambda b, s, *_: (0, 0))]
    for at, pieces in zip(starts, sets):
        last = pieces[0].shape[0] - 1
        args += pieces
        specs += [
            pl.BlockSpec((1, ks, n, width), lambda b, s, *_, at=at, last=last: (jnp.clip(b - at, 0, last), 0, 0, 0))
        ] * len(pieces)
    if added is not None:
        args.append(added)
        specs.append(pl.BlockSpec((1, tall, width), lambda b, s, *_: (added_at(b), s + first, 0)))
    scratch = [pltpu.VMEM((depth, width), jnp.bfloat16)] * 2
    alias = {}
    out_specs, out_shape = [], []
    if mode == "own":
        scratch += [pltpu.VMEM(block.shape[1:], jnp.float32), pltpu.SemaphoreType.DMA((1,))]
    if mode == "mine":
        args.append(out)
        specs.append(HBM)
        alias = {len(args) - 1: 0}
        out_specs = [pl.BlockSpec((i_own, 1, 128, width), lambda b, s, keys, _: (0, keys[1 + b], 0, 0))]
        out_shape = [jax.ShapeDtypeStruct(out.shape, out.dtype)]
    elif mode == "own" or gots:
        args += [*[g for g, _, _ in gots], out]
        specs += [place_spec(g) for g, _, _ in gots] + [HBM]
        alias = {len(args) - 1: 0}
        scratch.append(pltpu.SemaphoreType.DMA((max(len(gots), 1),)))
        out_specs, out_shape = [HBM], [jax.ShapeDtypeStruct(out.shape, out.dtype)]
    if mode in ("own", "send"):
        out_specs, out_shape = out_specs + [block_spec], out_shape + [block]
    elif mode == "lent":
        out_specs, out_shape = [block_spec, block_spec], [block, block]
    elif mode == "part":
        out_specs, out_shape = out_specs + [part_spec], out_shape + [jax.ShapeDtypeStruct((count, size, width), jnp.float32)]
    return pl.pallas_call(
        functools.partial(product_kernel, chunks, starts, [g.shape[0] for g, _, _ in gots], mode, added is not None),
        grid_spec=pltpu.PrefetchScalarGridSpec(
            num_scalar_prefetch=2, grid=(count, tiles), in_specs=specs, out_specs=out_specs, scratch_shapes=scratch
        ),
        out_shape=out_shape,
        input_output_aliases=alias,
        compiler_params=pltpu.CompilerParams(vmem_limit_bytes=VMEM + 12 * 2**20 if mode in ("mine", "send") else VMEM if len(sets) > 1 else 3 * VMEM // 4),
        cost_estimate=pl.CostEstimate(
            flops=6 * count * size * depth * width // (2 // tiles),
            bytes_accessed=4 * count * (size * (depth + width) + depth * width),
            transcendentals=0,
        ),
    )(*args)


def place_kernel(blocks, keys, *refs):
    gots, out, sem = refs[: len(blocks)], refs[len(blocks) + 1], refs[len(blocks) + 2]
    for act in ("start", "wait"):
        each_place(act, gots, blocks, out, keys, 0, pl.program_id(0), sem)


def place(out, gots):
    keys = jnp.stack([jnp.asarray(v, jnp.int32) for v in place_keys(gots)])
    blocks = [g.shape[0] for g, _, _ in gots]
    return pl.pallas_call(
        functools.partial(place_kernel, blocks),
        grid_spec=pltpu.PrefetchScalarGridSpec(
            num_scalar_prefetch=1,
            grid=(max(blocks),),
            in_specs=[place_spec(g) for g, _, _ in gots] + [HBM],
            out_specs=HBM,
            scratch_shapes=[pltpu.SemaphoreType.DMA((len(gots),))],
        ),
        out_shape=jax.ShapeDtypeStruct(out.shape, out.dtype),
        input_output_aliases={len(gots) + 1: 0},
        compiler_params=pltpu.CompilerParams(vmem_limit_bytes=VMEM // 2),
    )(keys, *[g for g, _, _ in gots], out)


def finish_kernel(keys, got, _, out):
    out[:, 0] = got[0]


def finish(out, got, js):
    rows_i, _, rows_a, width = out.shape
    return pl.pallas_call(
        finish_kernel,
        grid_spec=pltpu.PrefetchScalarGridSpec(
            num_scalar_prefetch=1,
            grid=(got.shape[0],),
            in_specs=[pl.BlockSpec((1, *got.shape[1:]), lambda b, _: (b, 0, 0, 0)), HBM],
            out_specs=pl.BlockSpec((rows_i, 1, rows_a, width), lambda b, keys: (0, keys[b], 0, 0)),
        ),
        out_shape=jax.ShapeDtypeStruct(out.shape, out.dtype),
        input_output_aliases={2: 0},
        compiler_params=pltpu.CompilerParams(vmem_limit_bytes=VMEM // 2),
    )(jnp.stack(js), got, out)


def hop(value, mask=0, planes=None, core=0):
    planes = {z: z for z in range(4)} if planes is None else planes
    flip = 2 * mask + core
    pairs = [(r * 4 + z, (r ^ flip) * 4 + w) for r in range(8) for z, w in planes.items()]
    return lax.ppermute(value, AXES, pairs)


def hop_middle(value):
    pairs = [(r * 4 + z, r * 4 + 3 - z) for r in range(8) for z in (1, 2)]
    pairs += [(r * 4 + z, (r ^ 1) * 4 + z) for r in range(8) for z in (0, 3)]
    return lax.ppermute(value, AXES, pairs)


def together(values):
    return lax.optimization_barrier(values)


def body(amplitudes, integrals, occ_energy, vir_energy):
    row, plane = lax.axis_index("row"), lax.axis_index("col")
    core, chip = lax.rem(row, 2), lax.div(row, 2)
    rows_i, ks, rows_a, depth = amplitudes.shape
    cols_j, cols_b = integrals.shape[2:]
    parts = cols_j // 2
    swap = {0: 1, 1: 0, 2: 3, 3: 2}
    is_end = (plane == 0) | (plane == 3)
    is_mid = ~is_end
    vir = vir_energy.reshape(1, -1)

    def share(plane_of):
        occ = [lax.dynamic_slice_in_dim(occ_energy, r * rows_i, rows_i, 0) for r in (row, row ^ 1)]
        part = lax.dynamic_slice_in_dim(vir_energy, plane_of * rows_a, rows_a, 0)
        rowd = (jnp.concatenate(occ)[:, None] - part[None, :]).reshape(-1, 1)
        return jnp.broadcast_to(rowd, (rowd.shape[0], 128))

    def column(w, pair, of_core):
        return (plane ^ w) * cols_j + of_core * parts + 2 * pair

    def either(at_end, at_mid):
        return jnp.where(is_end, at_end, at_mid)

    def along(x, y, z, mid=None, flip=0):
        got = [hop_middle(mid)] if mid is not None else []
        return [hop(x, mask=1), hop(y, mask=2), hop(z, planes=swap, core=flip)] + got

    room = (rows_i, occ_energy.shape[0], rows_a, cols_b)
    mine, other = columns(integrals, core, 0)
    a0, out = merge(mine, hop(other, core=1), core, room)
    state = dict(out=out, gots=[], sends=[])

    def columns_of(w, pair, of_core):
        at = column(w, pair, of_core)
        return [at, at + 1]

    def work(rows_in, sets, where, run=1, **how):
        js = [j for w, pair in where for j in columns_of(w, pair, core)]
        state["out"], send = product(rows_in, sets, run, js, occ_energy, vir, out=state["out"], gots=state["gots"], **how)
        state["gots"] = []
        state["sends"].append((send, [j for w, pair in where for j in columns_of(w, pair, 1 - core)], run))

    def begin(here, sets, where, chunks=(0, 1, 2)):
        js = [j for w, pair in where for j in columns_of(w, pair, core)]
        how = dict(mode="part", chunks=chunks)
        if state["gots"]:
            state["out"], sums = product(
                here, sets, 1, js, occ_energy, vir, out=state["out"], gots=state["gots"], **how
            )
            state["gots"] = []
            return sums
        (sums,) = product(here, sets, 1, js, occ_energy, vir, **how)
        return sums

    def exchange():
        now, state["sends"] = state["sends"], []
        return [(hop(v, core=1), js, keep) for v, js, keep in now]

    def end_round(values, moved=()):
        gots, sends = state["gots"] + list(moved), state["sends"]
        values, new_gots, new_sends, state["out"] = together(
            (values, [g[0] for g in gots], [s[0] for s in sends], state["out"])
        )
        state["gots"] = [(v, *g[1:]) for v, g in zip(new_gots, gots)]
        state["sends"] = [(v, *s[1:]) for v, s in zip(new_sends, sends)]
        return values

    a0x, a0y, a1, a3m = along(a0, a0, a0, a0)
    mine, other = columns(integrals, core, 1)
    (b0,) = merge(mine, hop(other, core=1), core)
    z = either(b0, a3m)
    v = end_round((amplitudes, a0, b0, a0x, a0y, a1, a3m, z))
    amplitudes, a0, b0, a0x, a0y, a1, a3m, z = v
    a_other = hop(amplitudes, core=1)
    a0d, b0y, ab, a2m = along(a0y, b0, z, a1)
    z = either(amplitudes[:2], a2m)
    e3 = either(ab, a2m)
    v = end_round((amplitudes, a_other, a0, b0, a0x, a0y, a0d, a1, a3m, b0y, ab, e3, z))
    amplitudes, a_other, a0, b0, a0x, a0y, a0d, a1, a3m, b0y, ab, e3, z = v
    b0x, e3y, first, b3m = along(b0, e3, z, b0)
    here = (*rows([amplitudes, a_other], chip), share(plane))
    work(here, [(a0, a0x, a0y, a0d)], [(0, 0)])
    z = either(amplitudes[2:], b3m)
    first, state["out"] = together((first, state["out"]))
    first_other = hop(first, core=1)
    v = end_round((here, a0, b0, a0x, a0y, a0d, a1, a3m, b0x, b0y, ab, e3, e3y, first, first_other, b3m, z))
    here, a0, b0, a0x, a0y, a0d, a1, a3m, b0x, b0y, ab, e3, e3y, first, first_other, b3m, z = v
    moved = exchange()
    e3x, b0d, second, b2m = along(e3, b0x, z, ab)
    e6, here = together((either(first, ab), here))
    b_sum = begin(here, [(b0, b0x, b0y)], [(0, 1)])
    z = either(a0x, b2m)
    v = (here, a0, b0, a0x, a0y, a0d, a1, a3m, b0x, b0y, b0d, b2m, b_sum, e3, e3x, e3y, e6, first, first_other, second, b3m, z)
    v = end_round(v, moved)
    here, a0, b0, a0x, a0y, a0d, a1, a3m, b0x, b0y, b0d, b2m, b_sum, e3, e3x, e3y, e6, first, first_other, second, b3m, z = v
    second_other = hop(second, core=1)
    e6x, e6y, third, g3x = along(e6, e6, z, a0x)
    e4, first = together((either(second, b2m), first))
    near = (*rows([first, second, first_other, second_other], chip), share(plane ^ 1))
    s_a, l_a = product(near, [(a0, a0x, a0y, a0d)], is_mid, columns_of(0, 0, core), occ_energy, vir, mode="lent")
    z = either(a0y, s_a)
    v = (here, near, a1, a3m, b0, b0x, b0y, b0d, a0y, a0d, b3m, b_sum, e3, e3x, e3y, e4, e6, e6x, e6y, third, g3x, l_a, z)
    v = end_round(v)
    here, near, a1, a3m, b0, b0x, b0y, b0d, a0y, a0d, b3m, b_sum, e3, e3x, e3y, e4, e6, e6x, e6y, third, g3x, l_a, z = v
    e3d, e6d, fourth, g3y = along(e3y, e6x, z, a0y)
    e5, near = together((either(third, b3m), near))
    s_b, l_b = product(near, [(b0, b0x, b0y, b0d)], is_mid, columns_of(0, 1, core), occ_energy, vir, mode="lent")
    z, here = together((either(a0d, s_b), here))
    work(here, [(b0d,)], [(0, 1)], chunks=(3,), added=b_sum)
    v = (here, a1, a3m, a0d, e3, e3x, e3y, e3d, e4, e5, e6, e6x, e6y, e6d, third, fourth, g3x, g3y, l_a, l_b, z)
    v = end_round(v)
    here, a1, a3m, a0d, e3, e3x, e3y, e3d, e4, e5, e6, e6x, e6y, e6d, third, fourth, g3x, g3y, l_a, l_b, z = v
    state["gots"].append((fourth, columns_of(1, 0, core), is_end))
    moved = exchange()
    e4x, e4y, fifth, g3d = along(e4, e4, z, a0d)
    work(here, [(e3, e3x, e3y, e3d), (e6, e6x, e6y, e6d)], [(2, 0), (either(3, 1), either(0, 1))])
    v = end_round((here, a1, a3m, e4, e4x, e4y, e5, third, fourth, fifth, g3x, g3y, g3d, l_a, l_b), moved)
    here, a1, a3m, e4, e4x, e4y, e5, third, fourth, fifth, g3x, g3y, g3d, l_a, l_b = v
    state["gots"].append((fifth, columns_of(1, 1, core), is_end))
    moved = exchange()
    e5x, e5y, sixth = along(e5, e5, l_a, flip=1)
    work(here, [(a1, third, fourth, fifth), (a3m, g3x, g3y, g3d)], [(1, 0), (3, 0)], is_mid)
    moved.append((sixth, columns_of(1, 0, 1 - core), is_end))
    v = end_round((here, e4, e4x, e4y, e5, e5x, e5y, l_b), moved)
    here, e4, e4x, e4y, e5, e5x, e5y, l_b = v
    moved = exchange()
    e4d, e5d, seventh = along(e4y, e5x, l_b, flip=1)
    last = [(2, 1), (3, 1)]
    js, js_other = ([j for w, pair in last for j in columns_of(w, pair, c)] for c in (core, 1 - core))
    sums = begin(here, [(e4, e4x, e4y), (e5, e5x, e5y)], last)
    sums, state["out"] = together((sums, state["out"]))
    out = place(state["out"], moved)
    here, e4d, e5d, sums, seventh, out = together((here, e4d, e5d, sums, seventh, out))
    how = dict(chunks=(3,), added=sums)
    gots = [(seventh, columns_of(1, 1, 1 - core), is_end)]
    out, send = product(here, [(e4d,), (e5d,)], 1, js, occ_energy, vir, mode="send", out=out, gots=gots, **how)
    got = hop(send, core=1)
    (out,) = product(here, [(e4d,), (e5d,)], 1, js, occ_energy, vir, mode="mine", out=out, **how)
    return finish(out, got, js_other)


def solution(mesh):
    planned = mesh.shape["row"] == 8 and mesh.shape["col"] == 4
    return jax.shard_map(
        body if planned else streamed,
        mesh=mesh,
        in_specs=(P("row", None, "col", None), P(None, "row", "col", None), P(), P()),
        out_specs=P("row", None, "col", None),
        check_vma=False,
    )
```
